256 devices in a mesh: sub: 64 (over x, z, core), dom: 4 (over y).
Axes of the slice: x: 4, y: 4, z: 8, core: 2. Of those that a mesh axis runs over, the one named last changes fastest.
Arguments:
- fine_nodes: bfloat16 [4, 32768, 512], P('dom', 'sub'), may hold values from -6 to 6
- fine_edges: bfloat16 [4, 131072, 512], P('dom', 'sub'), may hold values from -6 to 6
- edge_source: int32 [4, 131072], P('dom', 'sub'), may hold values from 0 to 1023
- edge_target: int32 [4, 131072], P('dom', 'sub'), may hold values from 0 to 511
- edge_blocks: int32 [4, 64], P('dom', 'sub'), may hold values from 1 to 4, as said below
- send_rows: int32 [4, 256, 128], P('dom', 'sub'), may hold values from 0 to 511
- coarse_map: int32 [4, 32768], P('dom', 'sub'), may hold values from 0 to 2047, as said below
- coarse_edges: bfloat16 [4, 16384, 512], P('dom', 'sub'), may hold values from -6 to 6
- coarse_source: int32 [4, 16384], P('dom', 'sub'), may hold values from 0 to 2047
- coarse_target: int32 [4, 16384], P('dom', 'sub'), may hold values from 0 to 31
- edge_first: bfloat16 [2, 1536, 512], replicated, may hold values from -0.15625 to 0.15625
- edge_second: bfloat16 [2, 512, 512], replicated, may hold values from -0.25 to 0.25
- edge_gain: bfloat16 [2, 512], replicated, may hold values from 0.5 to 1.5
- node_first: bfloat16 [2, 1024, 512], replicated, may hold values from -0.1875 to 0.1875
- node_second: bfloat16 [2, 512, 512], replicated, may hold values from -0.25 to 0.25
- node_gain: bfloat16 [2, 512], replicated, may hold values from 0.5 to 1.5
- lift_weight: bfloat16 [512, 512], replicated, may hold values from -0.25 to 0.25
Outputs:
- fine_out: bfloat16 [4, 32768, 512], P('dom', 'sub')
The draws below stay inside these ranges and needn't reach their ends.
Inputs may be any that keep to these rules, and one draw needn't show every extreme that they name: `edge_blocks`: used blocks of each device; some device uses all 4. `coarse_map`: A fine node held at subdomain s maps to a coarse node held at subdomain s - 1, s or s + 1 of its column.
All inputs are finite; a program needn't handle non-finite values.
Results may differ from the reference program's by a relative error of at most 0.014.
Values may be sent and summed in bfloat16 or wider, within the bound.
A program may use at most 64 MiB of HBM per device.

```python
import jax
import jax.numpy as jnp
from jax import lax

LATENT = 512
NODES_DEV = 512
BLOCKS = 4
COARSE_STEPS = 2
DOMS = 4
SUBS = 64
EDGE_BLOCK = 512
EDGES_DEV = 2048
HALO = 128
EXTENDED = 1024
COARSE_DEV = 32
COARSE_EDGES = 256
COLUMN = 32768
COARSE_COL = 2048


def draw_edge_blocks(key, part):
    key = jax.random.fold_in(key, 11)
    first_key, second_key, busy_key = jax.random.split(key, 3)
    first_factor = jax.random.randint(first_key, (DOMS * SUBS,), 0, 4)
    second_factor = jax.random.randint(second_key, (DOMS * SUBS,), 0, 4)
    counts = 1 + first_factor * second_factor * (BLOCKS - 1) // 9
    busiest = jax.random.randint(busy_key, (), 0, DOMS * SUBS)
    counts = jnp.where(jnp.arange(DOMS * SUBS) == busiest, BLOCKS, counts)
    return counts.reshape(DOMS, SUBS).astype(jnp.int32)


def draw_coarse_map(key, part):
    key = jax.random.fold_in(key, 23)
    shift_key, place_key = jax.random.split(key)
    home_sub = (jnp.arange(COLUMN) // NODES_DEV)[None, :]
    quarter = jax.random.randint(shift_key, (DOMS, COLUMN), 0, 4)
    offset = jnp.where(quarter == 0, -1, jnp.where(quarter == 3, 1, 0))
    owners = jnp.clip(home_sub + offset, 0, SUBS - 1)
    placed = jax.random.randint(place_key, (DOMS, COLUMN), 0, COARSE_DEV)
    targets = owners * COARSE_DEV + placed
    targets = targets.at[:, 0].set(0)
    targets = targets.at[:, COLUMN - 1].set(COARSE_COL - 1)
    return targets.astype(jnp.int32)


def with_ends(entries, rng, least, top_value):
    spot = [jax.random.randint(jax.random.fold_in(rng, axis), (), 0, length) for axis, length in enumerate(entries.shape)]
    widest = entries.shape.index(max(entries.shape))
    beside = spot[:widest] + [(spot[widest] + 1) % entries.shape[widest]] + spot[widest + 1:]
    return entries.at[tuple(spot)].set(least).at[tuple(beside)].set(top_value)


def levels(key, shape, shards, low, largest):
    factor_of, own = 1.0, jax.random.fold_in(key, 6)
    for dim, parts in shards:
        heights = jnp.exp(jax.random.uniform(jax.random.fold_in(own, dim), (parts,), jnp.float32, low / len(shards), largest / len(shards)))
        factor_of = factor_of * jnp.repeat(heights, shape[dim] // parts).reshape([-1 if axis == dim else 1 for axis in range(len(shape))])
    return factor_of


def noise(stream_key, extent, width, bound, cuts=(), kind=jnp.bfloat16):
    values = jax.random.normal(stream_key, extent, jnp.float32) * width
    if len(cuts) > 0:
        values = levels(stream_key, extent, cuts, -0.22, 0.18) * values
    return jnp.clip(values, min=-bound, max=bound).astype(kind)


def setup_inputs(seed: int = 0) -> dict:
    streams_of = jax.random.split(jax.random.key(seed), 18)
    fine_nodes = noise(streams_of[0], (DOMS, COLUMN, LATENT), 1.0, 6.0, ((0, 4), (1, 64)))
    fine_edges = noise(streams_of[1], (DOMS, SUBS * EDGES_DEV, LATENT), 1.0, 6.0, ((0, 4), (1, 64)))
    edge_source = with_ends(jax.random.randint(streams_of[2], (DOMS, SUBS * EDGES_DEV), 0, EXTENDED), jax.random.fold_in(streams_of[2], 1), 0, EXTENDED - 1).astype(jnp.int32)
    edge_target = with_ends(jax.random.randint(streams_of[3], (DOMS, SUBS * EDGES_DEV), 0, NODES_DEV), jax.random.fold_in(streams_of[3], 1), 0, NODES_DEV - 1).astype(jnp.int32)
    edge_blocks = draw_edge_blocks(jax.random.fold_in(streams_of[17], 71), 0)
    send_rows = with_ends(jax.random.randint(streams_of[5], (DOMS, 4 * SUBS, HALO), 0, NODES_DEV), jax.random.fold_in(streams_of[5], 1), 0, NODES_DEV - 1).astype(jnp.int32)
    coarse_map = draw_coarse_map(jax.random.fold_in(streams_of[17], 71), 0)
    coarse_edges = noise(streams_of[7], (DOMS, SUBS * COARSE_EDGES, LATENT), 1.0, 6.0, ((0, 4), (1, 64)))
    coarse_source = with_ends(jax.random.randint(streams_of[8], (DOMS, SUBS * COARSE_EDGES), 0, COARSE_COL), jax.random.fold_in(streams_of[8], 1), 0, COARSE_COL - 1).astype(jnp.int32)
    coarse_target = with_ends(jax.random.randint(streams_of[9], (DOMS, SUBS * COARSE_EDGES), 0, COARSE_DEV), jax.random.fold_in(streams_of[9], 1), 0, COARSE_DEV - 1).astype(jnp.int32)
    edge_first = noise(streams_of[10], (2, 3 * LATENT, LATENT), (3 * LATENT) ** -0.5, 0.15625)
    edge_second = noise(streams_of[11], (2, LATENT, LATENT), LATENT ** -0.5, 0.25)
    edge_gain = jnp.clip(1.0 + 0.1 * jax.random.normal(streams_of[12], (2, LATENT), jnp.float32), 0.5, 1.5).astype(jnp.bfloat16)
    node_first = noise(streams_of[13], (2, 2 * LATENT, LATENT), (2 * LATENT) ** -0.5, 0.1875)
    node_second = noise(streams_of[14], (2, LATENT, LATENT), LATENT ** -0.5, 0.25)
    node_gain = jnp.clip(1.0 + 0.1 * jax.random.normal(streams_of[15], (2, LATENT), jnp.float32), 0.5, 1.5).astype(jnp.bfloat16)
    lift_weight = noise(streams_of[16], (LATENT, LATENT), LATENT ** -0.5, 0.25)
    return {"fine_nodes": fine_nodes, "fine_edges": fine_edges, "edge_source": edge_source, "edge_target": edge_target, "edge_blocks": edge_blocks, "send_rows": send_rows, "coarse_map": coarse_map, "coarse_edges": coarse_edges, "coarse_source": coarse_source, "coarse_target": coarse_target, "edge_first": edge_first, "edge_second": edge_second, "edge_gain": edge_gain, "node_first": node_first, "node_second": node_second, "node_gain": node_gain, "lift_weight": lift_weight}


EPSILON = 1e-05

def layer_norm(values, scaling):
    centre = values - lax.optimization_barrier(jnp.mean(values, axis=-1, keepdims=True))
    variance = lax.optimization_barrier(jnp.mean(centre * centre, axis=-1, keepdims=True))
    return centre * lax.rsqrt(variance + EPSILON) * scaling.astype(jnp.float32)

def two_layer(pieces, weight_in, weight_out, scaling):
    joined = jnp.concatenate(pieces, axis=-1)
    hidden = jax.nn.silu(jnp.dot(joined, weight_in, preferred_element_type=jnp.float32)).astype(jnp.bfloat16)
    return layer_norm(jnp.dot(hidden, weight_out, preferred_element_type=jnp.float32), scaling)

def graph_layer(states, lookup, latents, sources, targets, usable, layer_index, weights):
    edge_first, edge_second, edge_gain, node_first, node_second, node_gain = weights
    message = two_layer([latents, lookup[sources], states[targets]], edge_first[layer_index], edge_second[layer_index], edge_gain[layer_index])
    renewed = (latents.astype(jnp.float32) + message).astype(jnp.bfloat16)
    masked = jnp.where(usable[:, None], renewed.astype(jnp.float32), jnp.float32(0.0))
    summed = jax.ops.segment_sum(masked, targets, num_segments=states.shape[0]).astype(jnp.bfloat16)
    update = two_layer([states, summed], node_first[layer_index], node_second[layer_index], node_gain[layer_index])
    return ((states.astype(jnp.float32) + update).astype(jnp.bfloat16), renewed)

def reference(fine_nodes, fine_edges, edge_source, edge_target, edge_blocks, send_rows, coarse_map, coarse_edges, coarse_source, coarse_target, edge_first, edge_second, edge_gain, node_first, node_second, node_gain, lift_weight):
    weights = (edge_first, edge_second, edge_gain, node_first, node_second, node_gain)
    states = fine_nodes.reshape(DOMS, SUBS, NODES_DEV, LATENT)
    send_lists = send_rows.reshape(DOMS, SUBS, 4, HALO)
    picked = jax.vmap(jax.vmap(lambda node_rows, chosen: node_rows[chosen]))(states, send_lists)
    vacant = jnp.zeros_like(picked[:, :1, 0])
    from_below = jnp.concatenate([vacant, picked[:, :-1, 1]], axis=1)
    from_above = jnp.concatenate([picked[:, 1:, 0], vacant], axis=1)
    vacant_dom = jnp.zeros_like(picked[:1, :, 0])
    from_left = jnp.concatenate([vacant_dom, picked[:-1, :, 3]], axis=0)
    from_right = jnp.concatenate([picked[1:, :, 2], vacant_dom], axis=0)
    tables = jnp.concatenate([states, from_below, from_above, from_left, from_right], axis=2)
    slot_block = (jnp.arange(EDGES_DEV) // EDGE_BLOCK).astype(jnp.int32)

    def fine_device(inputs):
        node_rows, lookup, latents, sources, targets, blocks = inputs
        result, unused = graph_layer(node_rows, lookup, latents, sources, targets, slot_block < blocks, 0, weights)
        return result
    refined = lax.map(fine_device, (states.reshape(DOMS * SUBS, NODES_DEV, LATENT), tables.reshape(DOMS * SUBS, EXTENDED, LATENT), fine_edges.reshape(DOMS * SUBS, EDGES_DEV, LATENT), edge_source.reshape(DOMS * SUBS, EDGES_DEV), edge_target.reshape(DOMS * SUBS, EDGES_DEV), edge_blocks.reshape(DOMS * SUBS))).reshape(DOMS, COLUMN, LATENT)

    def restrict(fine_column, targets):
        summed = jax.ops.segment_sum(fine_column.astype(jnp.float32), targets, num_segments=COARSE_COL)
        return (0.25 * summed).astype(jnp.bfloat16)
    coarse = jax.vmap(restrict)(refined, coarse_map)
    offsets = (jnp.arange(SUBS) * COARSE_DEV).astype(jnp.int32)
    global_targets = (coarse_target.reshape(DOMS, SUBS, COARSE_EDGES) + offsets[None, :, None]).reshape(DOMS, SUBS * COARSE_EDGES)

    def coarse_column(inputs):
        column, latents, sources, targets = inputs
        for repeat in range(COARSE_STEPS):
            column, latents = graph_layer(column, column, latents, sources, targets, targets >= 0, 1, weights)
        return column
    settled = lax.map(coarse_column, (coarse, coarse_edges, coarse_source, global_targets))

    def prolong(inputs):
        column, fine_column, targets = inputs
        lifted = jnp.dot(column[targets], lift_weight, preferred_element_type=jnp.float32)
        return (fine_column.astype(jnp.float32) + lifted).astype(jnp.bfloat16)
    return lax.map(prolong, (settled, refined, coarse_map))
```

```python
import functools

import jax
import jax.numpy as jnp
from jax import lax
from jax.experimental import pallas as pl
from jax.experimental.pallas import tpu as pltpu
from jax.sharding import PartitionSpec as P

EPSILON = 1e-05
BF = jnp.bfloat16
F32 = jnp.float32
MESH = pl.DeviceIdType.MESH
ORDER = (0, -1, 1, -2, 2, -3, 3, -4)
NX, NZ = 4, 8
GROUPS = ((0, 1), (1, 5), (5, 8))


def dot(a, b):
    return jnp.dot(a, b, preferred_element_type=F32)


def silu(v):
    return 0.5 * v * (1.0 + jnp.tanh(0.5 * v))


def layer_norm(v, gain):
    centre = v - jnp.mean(v, axis=-1, keepdims=True)
    variance = jnp.mean(centre * centre, axis=-1, keepdims=True)
    return centre * lax.rsqrt(variance + EPSILON) * gain


def column_of(row):
    n = row.shape[1]
    parts = [
        jnp.transpose(jnp.broadcast_to(row[:, i : i + 128], (128, 128))) for i in range(0, n, 128)
    ]
    return parts[0] if len(parts) == 1 else jnp.concatenate(parts, axis=0)


def ones_where(mask):
    return jnp.where(mask, 1.0, 0.0).astype(BF)


def pick_matrix(col, lanes, offset=0):
    reps = lanes // 128
    wide = col if reps == 1 else jnp.concatenate([col] * reps, axis=1)
    return ones_where(wide == lax.broadcasted_iota(jnp.int32, wide.shape, 1) + offset)


def sum_matrix(row, rows):
    shape = (rows, row.shape[1])
    return ones_where(jnp.broadcast_to(row, shape) == lax.broadcasted_iota(jnp.int32, shape, 0))


def kernel(
    fn, fe, es, et, eb, sr, cm, ce, cs, ct, ef, e2, eg, nf, n2, ng, lw,
    out,
    states, lat, wef, we2, wnf, wn2, wlw, cev,
    a_own, b_tgt, pick, halo, pre, src_col, tgt_col, agg, node_pre, refined,
    part, part_in, col0, col1, choice, choice_in, own, csrc, cs_other, sb, outv,
    load_sem, out_sem, halo_ss, halo_rs, part_ss, part_rs, ag_ss, ag_rs, set_ss, set_rs,
):
    s = lax.axis_index("sub")
    d = lax.axis_index("dom")
    subs = NX * NZ * 2
    x = s // (2 * NZ)
    z = lax.rem(s // 2, NZ)
    c = lax.rem(s, 2)
    s_up, s_down = lax.rem(s + 1, subs), lax.rem(s + subs - 1, subs)
    d_up, d_down = lax.rem(d + 1, 4), lax.rem(d + 3, 4)

    def place(xx, zz, cc):
        return xx * (2 * NZ) + zz * 2 + cc

    xs = [lax.rem(x + k, NX) for k in range(NX)]
    dev_z = {k: place(x, lax.rem(z + k + NZ, NZ), c) for k in (1, -1, 2, -2)}
    dev_x = [place(xs[k], z, c) for k in range(NX)]
    sibling = place(x, z, 1 - c)

    barrier = pltpu.get_barrier_semaphore()
    for partner in (s_up, s_down, *dev_z.values(), dev_x[1], dev_x[2], dev_x[3]):
        pl.semaphore_signal(barrier, inc=1, device_id={"sub": partner}, device_id_type=MESH)
    for partner in (d_up, d_down):
        pl.semaphore_signal(barrier, inc=1, device_id={"dom": partner}, device_id_type=MESH)

    pairs = [
        (fn.at[0], states),
        (ef.at[0], wef.at[0]),
        (fe.at[0], lat),
        (e2, we2),
        (nf.at[0], wnf.at[0]),
        (n2, wn2),
        (ce.at[0], cev),
        (ef.at[1], wef.at[1]),
        (nf.at[1], wnf.at[1]),
        (lw, wlw),
    ]
    loads = [pltpu.make_async_copy(a, b, load_sem.at[i]) for i, (a, b) in enumerate(pairs)]
    for copy in loads:
        copy.start()

    w = states.shape[1]
    nodes = states.shape[0]
    halo_rows = halo.shape[1]
    coarse = own.shape[0]
    c_edges = cev.shape[0]

    def remote(src, dst, ss, rs, sub=None, dom=None):
        device = {"sub": sub} if dom is None else {"dom": dom}
        return pltpu.make_async_remote_copy(
            src_ref=src, dst_ref=dst, send_sem=ss, recv_sem=rs,
            device_id=device, device_id_type=MESH,
        )

    loads[0].wait()
    loads[1].wait()
    a_own[...] = dot(states[...], wef[0, w : 2 * w]).astype(BF)
    listed = jnp.concatenate([column_of(sr[0, k : k + 1, :]) for k in range(4)], axis=0)
    picked = dot(pick_matrix(listed, nodes), a_own[...]).astype(BF)
    pick[...] = picked.reshape(4, halo_rows, w)
    pl.semaphore_wait(barrier, 11)
    halo_copies = [
        remote(pick.at[1], halo.at[0], halo_ss.at[0], halo_rs.at[0], sub=s_up),
        remote(pick.at[0], halo.at[1], halo_ss.at[1], halo_rs.at[1], sub=s_down),
        remote(pick.at[3], halo.at[2], halo_ss.at[2], halo_rs.at[2], dom=d_up),
        remote(pick.at[2], halo.at[3], halo_ss.at[3], halo_rs.at[3], dom=d_down),
    ]
    for copy in halo_copies:
        copy.start()
    cs_copy = remote(cs, cs_other, ag_ss.at[0, 21], ag_rs.at[0, 21], sub=sibling)
    cs_copy.start()

    b_tgt[...] = dot(states[...], wef[0, 2 * w : 3 * w]).astype(BF)
    edges = lat.shape[0]
    src_col[...] = column_of(es[...])
    tgt_col[...] = column_of(et[...])
    loads[2].wait()
    blocks = edges // nodes

    def first(b, carry):
        here = pl.ds(pl.multiple_of(b * nodes, nodes), nodes)
        pre[here, :] = (
            dot(lat[here, :], wef[0, 0:w])
            + dot(pick_matrix(src_col[here, :], nodes), a_own[...])
            + dot(pick_matrix(tgt_col[here, :], nodes), b_tgt[...])
        )
        return carry

    lax.fori_loop(0, blocks, first, 0)
    loads[4].wait()
    node_pre[...] = dot(states[...], wnf[0, 0:w])
    loads[3].wait()

    for copy in halo_copies:
        copy.wait()
    exists = (s > 0, s < subs - 1, d > 0, d < 3)
    for k in range(4):
        halo[k] = jnp.where(exists[k], halo[k].astype(F32), 0.0).astype(BF)
    agg[...] = jnp.zeros_like(agg)
    edge_gain = eg[...].astype(F32)
    node_gain = ng[...].astype(F32)
    used = eb[...]

    def second(b, carry):
        start = pl.multiple_of(b * nodes, nodes)
        here = pl.ds(start, nodes)
        table = halo[...].reshape(4 * halo_rows, w)
        v = pre[here, :] + dot(pick_matrix(src_col[here, :], 4 * halo_rows, nodes), table)
        message = layer_norm(dot(silu(v).astype(BF), we2[0]), edge_gain[0:1])
        renewed = (lat[here, :].astype(F32) + message).astype(BF)
        targets = jnp.where(b < used, et[:, here], -1)
        agg[...] += dot(sum_matrix(targets, nodes), renewed)
        return carry

    lax.fori_loop(0, blocks, second, 0)

    loads[5].wait()
    v = node_pre[...] + dot(agg[...].astype(BF), wnf[0, w : 2 * w])
    update = layer_norm(dot(silu(v).astype(BF), wn2[0]), node_gain[0:1])
    refined[...] = (states[...].astype(F32) + update).astype(BF)
    slots = cm[...] - (s - 1) * coarse
    partial = dot(sum_matrix(slots, 3 * coarse), refined[...])
    part[0] = partial[0:coarse].astype(BF)
    part[1] = partial[2 * coarse : 3 * coarse].astype(BF)
    part_copies = [
        remote(part.at[0], part_in.at[0], part_ss.at[0], part_rs.at[0], sub=s_down),
        remote(part.at[1], part_in.at[1], part_ss.at[1], part_rs.at[1], sub=s_up),
    ]
    for copy in part_copies:
        copy.start()
    csrc[0:c_edges, :] = column_of(cs[...])
    cs_copy.wait()
    csrc[c_edges:, :] = column_of(cs_other[...])
    tgt_pick = ones_where(
        column_of(ct[...])[:, 0:coarse]
        == lax.broadcasted_iota(jnp.int32, (c_edges, coarse), 1)
    )
    tgt_sum = sum_matrix(ct[...], coarse)
    for i in (6, 7, 8, 9):
        loads[i].wait()
    for copy in part_copies:
        copy.wait()
    own[...] = (
        0.25
        * (
            partial[coarse : 2 * coarse]
            + part_in[0].astype(F32)
            + part_in[1].astype(F32)
        )
    ).astype(BF)

    def gather_parts(g, col):
        ss = lambda i: ag_ss.at[g, i]
        rs = lambda i: ag_rs.at[g, i]

        def send(src, dst, i, target):
            return remote(src, dst, ss(i), rs(i), sub=target)

        def arrived(i, ref):
            remote(ref, ref, ss(i), rs(i), sub=sibling).wait_recv()

        def lines(k, q):
            return col.at[k, GROUPS[q][0] : GROUPS[q][1]]

        def z_send(k, i, step):
            offset = ORDER[i] - step
            to = ORDER.index(offset if offset < 4 else -4)
            return send(col.at[k, i], col.at[k, to], (32 if k else 0) + to, dev_z[step])

        def z_near(k):
            return [z_send(k, 0, step) for step in (1, -1, 2, -2)]

        def z_beyond(k, i):
            if i == 3:
                steps = (1,) if k else (1, 2)
            else:
                steps = (-1, -2) if k else (-1,)
            return [z_send(k, i, step) for step in steps]

        def x_sends(q):
            return [
                send(lines(0, q), lines(3, q), 8 + q, dev_x[1]),
                send(lines(0, q), lines(1, q), 12 + q, dev_x[3]),
            ]

        def x_far():
            return [send(col.at[0, 0], col.at[2, 0], 24, dev_x[2])]

        def choice_send():
            return [send(choice.at[g], choice_in.at[g], 20, sibling)]

        def start(copies):
            for copy in copies:
                copy.start()

        def z_arrived(k, i):
            arrived((32 if k else 0) + i, col.at[k, i])

        def begin():
            start(x_far() + z_near(0) + x_sends(0))

        def forward():
            for i in (3, 4):
                z_arrived(0, i)
                start(z_beyond(0, i))
            arrived(24, col.at[2, 0])
            start(z_near(2))
            for i in (1, 2):
                z_arrived(0, i)
            start(x_sends(1))
            for i in (3, 4):
                z_arrived(2, i)
                start(z_beyond(2, i))
            for i in (5, 6, 7):
                z_arrived(0, i)
            start(x_sends(2))

        def beside():
            for q in range(3):
                arrived(8 + q, lines(3, q))
                arrived(12 + q, lines(1, q))

        def far():
            for i in (1, 2, 5, 6, 7):
                z_arrived(2, i)

        def exchange(theirs):
            choice[g] = theirs
            start(choice_send())

        def exchanged():
            arrived(20, choice_in.at[g])
            return choice_in[g]

        def finish():
            copies = x_far() + choice_send()
            for q in range(3):
                copies += x_sends(q)
            for k in (0, 2):
                copies += z_near(k) + z_beyond(k, 3) + z_beyond(k, 4)
            for copy in copies:
                copy.wait_send()

        return begin, forward, beside, far, exchange, exchanged, finish

    lane = lax.broadcasted_iota(jnp.int32, (1, NZ * coarse), 1)
    turn = lane // coarse
    ahead = jnp.where(lax.rem(turn, 2) == 1, -((turn + 1) // 2), turn // 2)
    span = 2 * coarse
    line_ids = lax.rem(z + ahead + NZ, NZ) * span + c * coarse + lax.rem(lane, coarse)

    finishes = []
    for g, col in enumerate((col0, col1)):
        begin, forward, beside, far, exchange, exchanged, finish = gather_parts(g, col)
        mine = own[...]
        col[0, 0] = mine
        begin()
        picked_own = dot(tgt_pick, mine).astype(BF)
        c_pre = dot(cev[...], wef[1, 0:w]) + dot(picked_own, wef[1, 2 * w : 3 * w])
        n_pre = dot(mine, wnf[1, 0:w])

        def chosen_rows(k, rows):
            labels = jnp.concatenate([csrc[rows, :]] * (NZ * coarse // 128), axis=1)
            return dot(
                ones_where(labels == line_ids + xs[k] * (NZ * span)),
                col[k].reshape(NZ * coarse, w),
            )

        everyone = slice(0, 2 * c_edges)
        forward()
        fetched = chosen_rows(0, everyone)
        beside()
        fetched += chosen_rows(3, everyone) + chosen_rows(1, everyone)
        far()
        exchange((fetched[c_edges:] + chosen_rows(2, slice(c_edges, 2 * c_edges))).astype(BF))
        fetched = fetched[0:c_edges] + chosen_rows(2, slice(0, c_edges))
        fetched += exchanged().astype(F32)
        v = c_pre + dot(fetched.astype(BF), wef[1, w : 2 * w])
        message = layer_norm(dot(silu(v).astype(BF), we2[1]), edge_gain[1:2])
        new_edges = (cev[...].astype(F32) + message).astype(BF)
        cev[...] = new_edges
        summed = dot(tgt_sum, new_edges).astype(BF)
        v = n_pre + dot(summed, wnf[1, w : 2 * w])
        update = layer_norm(dot(silu(v).astype(BF), wn2[1]), node_gain[1:2])
        own[...] = (mine.astype(F32) + update).astype(BF)
        finishes.append(finish)

    sb[1] = own[...]
    sb[3] = jnp.zeros_like(sb[3])
    set_copies = [
        remote(sb.at[1], sb.at[0], set_ss.at[0], set_rs.at[0], sub=s_up),
        remote(sb.at[1], sb.at[2], set_ss.at[1], set_rs.at[1], sub=s_down),
    ]
    for copy in set_copies:
        copy.start()
    chosen = pick_matrix(column_of(slots), 4 * coarse)
    for finish in finishes:
        finish()
    for copy in set_copies:
        copy.wait()
    lifted = dot(sb[...].reshape(4 * coarse, w), wlw[...])
    high = lifted.astype(BF)
    low = (lifted - high.astype(F32)).astype(BF)
    outv[...] = (refined[...].astype(F32) + dot(chosen, high) + dot(chosen, low)).astype(BF)
    copy = pltpu.make_async_copy(outv, out.at[0], out_sem)
    copy.start()
    copy.wait()


def per_device(*arrays):
    fn, fe = arrays[0], arrays[1]
    nodes, w = fn.shape[1], fn.shape[2]
    edges = fe.shape[1]
    halo_rows = arrays[5].shape[2]
    c_edges = arrays[7].shape[1]
    coarse = nodes // 16
    any_space = pl.BlockSpec(memory_space=pl.ANY)
    vmem = pl.BlockSpec(memory_space=pltpu.VMEM)
    big = {0, 1, 7, 10, 11, 13, 14, 16}
    specs = [any_space if i in big else vmem for i in range(17)]
    V = pltpu.VMEM
    D = pltpu.SemaphoreType.DMA
    scratch = [
        V((nodes, w), BF),
        V((edges, w), BF),
        V((2, 3 * w, w), BF),
        V((2, w, w), BF),
        V((2, 2 * w, w), BF),
        V((2, w, w), BF),
        V((w, w), BF),
        V((c_edges, w), BF),
        V((nodes, w), BF),
        V((nodes, w), BF),
        V((4, halo_rows, w), BF),
        V((4, halo_rows, w), BF),
        V((edges, w), F32),
        V((edges, 128), jnp.int32),
        V((edges, 128), jnp.int32),
        V((nodes, w), F32),
        V((nodes, w), F32),
        V((nodes, w), BF),
        V((2, coarse, w), BF),
        V((2, coarse, w), BF),
        V((NX, NZ, coarse, w), BF),
        V((NX, NZ, coarse, w), BF),
        V((2, c_edges, w), BF),
        V((2, c_edges, w), BF),
        V((coarse, w), BF),
        V((2 * c_edges, 128), jnp.int32),
        V((1, c_edges), jnp.int32),
        V((4, coarse, w), BF),
        V((nodes, w), BF),
        D((10,)),
        D,
        D((4,)),
        D((4,)),
        D((2,)),
        D((2,)),
        D((2, 40)),
        D((2, 40)),
        D((2,)),
        D((2,)),
    ]
    return pl.pallas_call(
        kernel,
        out_shape=jax.ShapeDtypeStruct((1, nodes, w), BF),
        in_specs=specs,
        out_specs=any_space,
        scratch_shapes=scratch,
        compiler_params=pltpu.CompilerParams(
            collective_id=0, has_side_effects=True, vmem_limit_bytes=56 * 1024 * 1024
        ),
        cost_estimate=pl.CostEstimate(
            flops=9_000_000_000, bytes_accessed=12_000_000, transcendentals=2_000_000
        ),
    )(*arrays)


def solution(mesh):
    row = P("dom", "sub")
    wide = P("dom", "sub", None)
    placed = (
        wide, wide, row, row, row, wide, row, wide, row, row,
        P(), P(), P(), P(), P(), P(), P(),
    )
    return jax.shard_map(
        per_device, mesh=mesh, in_specs=placed, out_specs=wide, check_vma=False
    )
```

```python
import functools

import jax
import jax.numpy as jnp
from jax import lax
from jax.experimental import pallas as pl
from jax.experimental.pallas import tpu as pltpu
from jax.sharding import PartitionSpec as P

EPSILON = 1e-05
BF = jnp.bfloat16
F32 = jnp.float32
MESH = pl.DeviceIdType.MESH
ORDER = (0, -1, 1, -2, 2, -3, 3, -4)
NX, NZ = 4, 8
GROUPS = ((0, 1), (1, 5), (5, 8))


def dot(a, b):
    return jnp.dot(a, b, preferred_element_type=F32)


def silu(v):
    return 0.5 * v * (1.0 + jnp.tanh(0.5 * v))


def layer_norm(v, gain):
    centre = v - jnp.mean(v, axis=-1, keepdims=True)
    variance = jnp.mean(centre * centre, axis=-1, keepdims=True)
    return centre * lax.rsqrt(variance + EPSILON) * gain


def column_of(row):
    n = row.shape[1]
    parts = [
        jnp.transpose(jnp.broadcast_to(row[:, i : i + 128], (128, 128))) for i in range(0, n, 128)
    ]
    return parts[0] if len(parts) == 1 else jnp.concatenate(parts, axis=0)


def ones_where(mask):
    return jnp.where(mask, 1.0, 0.0).astype(BF)


def pick_matrix(col, lanes, offset=0):
    reps = lanes // 128
    wide = col if reps == 1 else jnp.concatenate([col] * reps, axis=1)
    return ones_where(wide == lax.broadcasted_iota(jnp.int32, wide.shape, 1) + offset)


def sum_matrix(row, rows):
    shape = (rows, row.shape[1])
    return ones_where(jnp.broadcast_to(row, shape) == lax.broadcasted_iota(jnp.int32, shape, 0))


def kernel(
    fn, fe, es_far, et_far, eb, sr_far, cm_far, ce, cs_far, ct_far, ef, e2, eg_far, nf, n2, ng_far, lw,
    out,
    es, et, sr, cm, cs, ct, eg, ng,
    states, lat, wef, we2, wnf, wn2, wlw, cev,
    a_own, b_tgt, pick, halo, pre, src_col, tgt_col, agg, node_pre, refined,
    part, part_in, col0, col1, choice, choice_in, own, csrc, cs_other, sb, outv,
    load_sem, label_sem, out_sem, halo_ss, halo_rs, part_ss, part_rs, ag_ss, ag_rs, set_ss, set_rs,
):
    s = lax.axis_index("sub")
    d = lax.axis_index("dom")
    subs = NX * NZ * 2
    x = s // (2 * NZ)
    z = lax.rem(s // 2, NZ)
    c = lax.rem(s, 2)
    s_up, s_down = lax.rem(s + 1, subs), lax.rem(s + subs - 1, subs)
    d_up, d_down = lax.rem(d + 1, 4), lax.rem(d + 3, 4)

    def place(xx, zz, cc):
        return xx * (2 * NZ) + zz * 2 + cc

    xs = [lax.rem(x + k, NX) for k in range(NX)]
    dev_z = {k: place(x, lax.rem(z + k + NZ, NZ), c) for k in (1, -1, 2, -2)}
    dev_x = [place(xs[k], z, c) for k in range(NX)]
    sibling = place(x, z, 1 - c)

    barrier = pltpu.get_barrier_semaphore()
    for partner in (s_up, s_down, *dev_z.values(), dev_x[1], dev_x[2], dev_x[3]):
        pl.semaphore_signal(barrier, inc=1, device_id={"sub": partner}, device_id_type=MESH)
    for partner in (d_up, d_down):
        pl.semaphore_signal(barrier, inc=1, device_id={"dom": partner}, device_id_type=MESH)

    labels = [
        pltpu.make_async_copy(a, b, label_sem.at[i])
        for i, (a, b) in enumerate(
            [
                (sr_far, sr), (es_far, es), (et_far, et), (cs_far, cs),
                (cm_far, cm), (ct_far, ct), (eg_far, eg), (ng_far, ng),
            ]
        )
    ]
    pairs = [
        (fn.at[0], states),
        (ef.at[0], wef.at[0]),
        (fe.at[0], lat),
        (e2, we2),
        (nf.at[0], wnf.at[0]),
        (n2, wn2),
        (ce.at[0], cev),
        (ef.at[1], wef.at[1]),
        (nf.at[1], wnf.at[1]),
        (lw, wlw),
    ]
    loads = [pltpu.make_async_copy(a, b, load_sem.at[i]) for i, (a, b) in enumerate(pairs)]
    for copy in loads[:2] + labels + loads[2:]:
        copy.start()

    w = states.shape[1]
    nodes = states.shape[0]
    halo_rows = halo.shape[1]
    coarse = own.shape[0]
    c_edges = cev.shape[0]

    def remote(src, dst, ss, rs, sub=None, dom=None):
        device = {"sub": sub} if dom is None else {"dom": dom}
        return pltpu.make_async_remote_copy(
            src_ref=src, dst_ref=dst, send_sem=ss, recv_sem=rs,
            device_id=device, device_id_type=MESH,
        )

    loads[0].wait()
    loads[1].wait()
    a_own[...] = dot(states[...], wef[0, w : 2 * w]).astype(BF)
    for copy in labels:
        copy.wait()
    listed = jnp.concatenate([column_of(sr[0, k : k + 1, :]) for k in range(4)], axis=0)
    picked = dot(pick_matrix(listed, nodes), a_own[...]).astype(BF)
    pick[...] = picked.reshape(4, halo_rows, w)
    pl.semaphore_wait(barrier, 11)
    halo_copies = [
        remote(pick.at[1], halo.at[0], halo_ss.at[0], halo_rs.at[0], sub=s_up),
        remote(pick.at[0], halo.at[1], halo_ss.at[1], halo_rs.at[1], sub=s_down),
        remote(pick.at[3], halo.at[2], halo_ss.at[2], halo_rs.at[2], dom=d_up),
        remote(pick.at[2], halo.at[3], halo_ss.at[3], halo_rs.at[3], dom=d_down),
    ]
    for copy in halo_copies:
        copy.start()
    cs_copy = remote(cs, cs_other, ag_ss.at[0, 21], ag_rs.at[0, 21], sub=sibling)
    cs_copy.start()

    b_tgt[...] = dot(states[...], wef[0, 2 * w : 3 * w]).astype(BF)
    edges = lat.shape[0]
    src_col[...] = column_of(es[...])
    tgt_col[...] = column_of(et[...])
    loads[2].wait()
    blocks = edges // nodes

    def first(b, carry):
        here = pl.ds(pl.multiple_of(b * nodes, nodes), nodes)
        pre[here, :] = (
            dot(lat[here, :], wef[0, 0:w])
            + dot(pick_matrix(src_col[here, :], nodes), a_own[...])
            + dot(pick_matrix(tgt_col[here, :], nodes), b_tgt[...])
        )
        return carry

    lax.fori_loop(0, blocks, first, 0, unroll=True)
    loads[4].wait()
    node_pre[...] = dot(states[...], wnf[0, 0:w])
    loads[3].wait()

    for copy in halo_copies:
        copy.wait()
    exists = (s > 0, s < subs - 1, d > 0, d < 3)
    for k in range(4):
        halo[k] = jnp.where(exists[k], halo[k].astype(F32), 0.0).astype(BF)
    agg[...] = jnp.zeros_like(agg)
    edge_gain = eg[...].astype(F32)
    node_gain = ng[...].astype(F32)
    used = eb[...]

    def second(b, carry):
        start = pl.multiple_of(b * nodes, nodes)
        here = pl.ds(start, nodes)
        table = halo[...].reshape(4 * halo_rows, w)
        v = pre[here, :] + dot(pick_matrix(src_col[here, :], 4 * halo_rows, nodes), table)
        message = layer_norm(dot(silu(v).astype(BF), we2[0]), edge_gain[0:1])
        renewed = (lat[here, :].astype(F32) + message).astype(BF)
        targets = jnp.where(b < used, et[:, here], -1)
        agg[...] += dot(sum_matrix(targets, nodes), renewed)
        return carry

    lax.fori_loop(0, blocks, second, 0, unroll=True)

    loads[5].wait()
    v = node_pre[...] + dot(agg[...].astype(BF), wnf[0, w : 2 * w])
    update = layer_norm(dot(silu(v).astype(BF), wn2[0]), node_gain[0:1])
    refined[...] = (states[...].astype(F32) + update).astype(BF)
    slots = cm[...] - (s - 1) * coarse
    partial = dot(sum_matrix(slots, 3 * coarse), refined[...])
    part[0] = partial[0:coarse].astype(BF)
    part[1] = partial[2 * coarse : 3 * coarse].astype(BF)
    part_copies = [
        remote(part.at[0], part_in.at[0], part_ss.at[0], part_rs.at[0], sub=s_down),
        remote(part.at[1], part_in.at[1], part_ss.at[1], part_rs.at[1], sub=s_up),
    ]
    for copy in part_copies:
        copy.start()
    csrc[0:c_edges, :] = column_of(cs[...])
    cs_copy.wait()
    csrc[c_edges:, :] = column_of(cs_other[...])
    tgt_pick = ones_where(
        column_of(ct[...])[:, 0:coarse]
        == lax.broadcasted_iota(jnp.int32, (c_edges, coarse), 1)
    )
    tgt_sum = sum_matrix(ct[...], coarse)
    for i in (6, 7, 8, 9):
        loads[i].wait()
    for copy in part_copies:
        copy.wait()
    own[...] = (
        0.25
        * (
            partial[coarse : 2 * coarse]
            + part_in[0].astype(F32)
            + part_in[1].astype(F32)
        )
    ).astype(BF)

    def gather_parts(g, col):
        ss = lambda i: ag_ss.at[g, i]
        rs = lambda i: ag_rs.at[g, i]

        def send(src, dst, i, target):
            return remote(src, dst, ss(i), rs(i), sub=target)

        def arrived(i, ref):
            remote(ref, ref, ss(i), rs(i), sub=sibling).wait_recv()

        def lines(k, q):
            return col.at[k, GROUPS[q][0] : GROUPS[q][1]]

        def z_send(k, i, step):
            offset = ORDER[i] - step
            to = ORDER.index(offset if offset < 4 else -4)
            return send(col.at[k, i], col.at[k, to], (32 if k else 0) + to, dev_z[step])

        def z_near(k):
            return [z_send(k, 0, step) for step in (2, -2, 1, -1)]

        def z_beyond(k, i):
            if i == 3:
                steps = (1,) if k else (2, 1)
            else:
                steps = (-2, -1) if k else (-1,)
            return [z_send(k, i, step) for step in steps]

        def x_sends(q):
            return [
                send(lines(0, q), lines(3, q), 8 + q, dev_x[1]),
                send(lines(0, q), lines(1, q), 12 + q, dev_x[3]),
            ]

        def x_far():
            return [send(col.at[0, 0], col.at[2, 0], 24, dev_x[2])]

        def choice_send():
            return [send(choice.at[g], choice_in.at[g], 20, sibling)]

        def start(copies):
            for copy in copies:
                copy.start()

        def z_arrived(k, i):
            arrived((32 if k else 0) + i, col.at[k, i])

        def begin():
            start(x_far() + z_near(0) + x_sends(0))

        def forward():
            for i in (3, 4):
                z_arrived(0, i)
                start(z_beyond(0, i))
            arrived(24, col.at[2, 0])
            start(z_near(2))
            for i in (1, 2):
                z_arrived(0, i)
            start(x_sends(1))
            for i in (3, 4):
                z_arrived(2, i)
                start(z_beyond(2, i))
            for i in (5, 6, 7):
                z_arrived(0, i)
            start(x_sends(2))

        def beside():
            for q in range(3):
                arrived(8 + q, lines(3, q))
                arrived(12 + q, lines(1, q))

        def far():
            for i in (1, 2, 5, 6, 7):
                z_arrived(2, i)

        def exchange(theirs):
            choice[g] = theirs
            start(choice_send())

        def exchanged():
            arrived(20, choice_in.at[g])
            return choice_in[g]

        def finish():
            copies = x_far() + choice_send()
            for q in range(3):
                copies += x_sends(q)
            for k in (0, 2):
                copies += z_near(k) + z_beyond(k, 3) + z_beyond(k, 4)
            for copy in copies:
                copy.wait_send()

        return begin, forward, beside, far, exchange, exchanged, finish

    lane = lax.broadcasted_iota(jnp.int32, (1, NZ * coarse), 1)
    turn = lane // coarse
    ahead = jnp.where(lax.rem(turn, 2) == 1, -((turn + 1) // 2), turn // 2)
    span = 2 * coarse
    line_ids = lax.rem(z + ahead + NZ, NZ) * span + c * coarse + lax.rem(lane, coarse)

    finishes = []
    for g, col in enumerate((col0, col1)):
        begin, forward, beside, far, exchange, exchanged, finish = gather_parts(g, col)
        mine = own[...]
        col[0, 0] = mine
        begin()
        picked_own = dot(tgt_pick, mine).astype(BF)
        c_pre = dot(cev[...], wef[1, 0:w]) + dot(picked_own, wef[1, 2 * w : 3 * w])
        n_pre = dot(mine, wnf[1, 0:w])

        def chosen_rows(k, rows):
            labels = jnp.concatenate([csrc[rows, :]] * (NZ * coarse // 128), axis=1)
            return dot(
                ones_where(labels == line_ids + xs[k] * (NZ * span)),
                col[k].reshape(NZ * coarse, w),
            )

        everyone = slice(0, 2 * c_edges)
        forward()
        fetched = chosen_rows(0, everyone)
        beside()
        fetched += chosen_rows(3, everyone) + chosen_rows(1, everyone)
        far()
        exchange((fetched[c_edges:] + chosen_rows(2, slice(c_edges, 2 * c_edges))).astype(BF))
        fetched = fetched[0:c_edges] + chosen_rows(2, slice(0, c_edges))
        fetched += exchanged().astype(F32)
        v = c_pre + dot(fetched.astype(BF), wef[1, w : 2 * w])
        message = layer_norm(dot(silu(v).astype(BF), we2[1]), edge_gain[1:2])
        new_edges = (cev[...].astype(F32) + message).astype(BF)
        cev[...] = new_edges
        summed = dot(tgt_sum, new_edges).astype(BF)
        v = n_pre + dot(summed, wnf[1, w : 2 * w])
        update = layer_norm(dot(silu(v).astype(BF), wn2[1]), node_gain[1:2])
        own[...] = (mine.astype(F32) + update).astype(BF)
        finishes.append(finish)

    sb[1] = own[...]
    sb[3] = jnp.zeros_like(sb[3])
    set_copies = [
        remote(sb.at[1], sb.at[0], set_ss.at[0], set_rs.at[0], sub=s_up),
        remote(sb.at[1], sb.at[2], set_ss.at[1], set_rs.at[1], sub=s_down),
    ]
    for copy in set_copies:
        copy.start()
    chosen = pick_matrix(column_of(slots), 4 * coarse)
    for finish in finishes:
        finish()
    for copy in set_copies:
        copy.wait()
    lifted = dot(sb[...].reshape(4 * coarse, w), wlw[...])
    high = lifted.astype(BF)
    low = (lifted - high.astype(F32)).astype(BF)
    halves = []
    for i in range(2):
        rows = slice(i * (nodes // 2), (i + 1) * (nodes // 2))
        outv[rows, :] = (
            refined[rows, :].astype(F32) + dot(chosen[rows], high) + dot(chosen[rows], low)
        ).astype(BF)
        halves.append(pltpu.make_async_copy(outv.at[rows], out.at[0, rows], out_sem.at[i]))
        halves[i].start()
    for copy in halves:
        copy.wait()


def per_device(*arrays):
    fn, fe = arrays[0], arrays[1]
    nodes, w = fn.shape[1], fn.shape[2]
    edges = fe.shape[1]
    halo_rows = arrays[5].shape[2]
    c_edges = arrays[7].shape[1]
    coarse = nodes // 16
    far = pl.BlockSpec(memory_space=pl.ANY)
    near = pl.BlockSpec(memory_space=pltpu.VMEM)
    specs = [near if i == 4 else far for i in range(17)]
    V = pltpu.VMEM
    D = pltpu.SemaphoreType.DMA
    scratch = [
        V((1, edges), jnp.int32),
        V((1, edges), jnp.int32),
        V((1, 4, halo_rows), jnp.int32),
        V((1, nodes), jnp.int32),
        V((1, c_edges), jnp.int32),
        V((1, c_edges), jnp.int32),
        V((2, w), BF),
        V((2, w), BF),
        V((nodes, w), BF),
        V((edges, w), BF),
        V((2, 3 * w, w), BF),
        V((2, w, w), BF),
        V((2, 2 * w, w), BF),
        V((2, w, w), BF),
        V((w, w), BF),
        V((c_edges, w), BF),
        V((nodes, w), BF),
        V((nodes, w), BF),
        V((4, halo_rows, w), BF),
        V((4, halo_rows, w), BF),
        V((edges, w), F32),
        V((edges, 128), jnp.int32),
        V((edges, 128), jnp.int32),
        V((nodes, w), F32),
        V((nodes, w), F32),
        V((nodes, w), BF),
        V((2, coarse, w), BF),
        V((2, coarse, w), BF),
        V((NX, NZ, coarse, w), BF),
        V((NX, NZ, coarse, w), BF),
        V((2, c_edges, w), BF),
        V((2, c_edges, w), BF),
        V((coarse, w), BF),
        V((2 * c_edges, 128), jnp.int32),
        V((1, c_edges), jnp.int32),
        V((4, coarse, w), BF),
        V((nodes, w), BF),
        D((10,)),
        D((8,)),
        D((2,)),
        D((4,)),
        D((4,)),
        D((2,)),
        D((2,)),
        D((2, 40)),
        D((2, 40)),
        D((2,)),
        D((2,)),
    ]
    return pl.pallas_call(
        kernel,
        out_shape=jax.ShapeDtypeStruct((1, nodes, w), BF),
        in_specs=specs,
        out_specs=far,
        scratch_shapes=scratch,
        compiler_params=pltpu.CompilerParams(
            collective_id=0, has_side_effects=True, vmem_limit_bytes=56 * 1024 * 1024
        ),
        cost_estimate=pl.CostEstimate(
            flops=9_000_000_000, bytes_accessed=12_000_000, transcendentals=2_000_000
        ),
    )(*arrays)


def solution(mesh):
    row = P("dom", "sub")
    wide = P("dom", "sub", None)
    placed = (
        wide, wide, row, row, row, wide, row, wide, row, row,
        P(), P(), P(), P(), P(), P(), P(),
    )
    return jax.shard_map(
        per_device, mesh=mesh, in_specs=placed, out_specs=wide, check_vma=False
    )
```

```python
import functools

import jax
import jax.numpy as jnp
from jax import lax
from jax.experimental import pallas as pl
from jax.experimental.pallas import tpu as pltpu
from jax.sharding import PartitionSpec as P

EPSILON = 1e-05
BF = jnp.bfloat16
F32 = jnp.float32
MESH = pl.DeviceIdType.MESH
ORDER = (0, -1, 1, -2, 2, -3, 3, -4)
NX, NZ = 4, 8
GROUPS = ((0, 1), (1, 5), (5, 8))


def dot(a, b):
    return jnp.dot(a, b, preferred_element_type=F32)


def silu(v):
    half = 0.5 * v
    return half + half * jnp.tanh(half)


def centred(weight):
    wide = weight.astype(F32)
    return (wide - jnp.mean(wide, axis=-1, keepdims=True)).astype(BF)


def scaled(centre, gain):
    variance = jnp.mean(centre * centre, axis=-1, keepdims=True)
    return centre * lax.rsqrt(variance + EPSILON) * gain


def column_of(row):
    n = row.shape[1]
    parts = [
        jnp.transpose(jnp.broadcast_to(row[:, i : i + 128], (128, 128))) for i in range(0, n, 128)
    ]
    return (parts[0] if len(parts) == 1 else jnp.concatenate(parts, axis=0)).astype(jnp.int16)


def ones_where(mask):
    return jnp.where(mask, jnp.ones((), BF), jnp.zeros((), BF))


def pick_matrix(col, lanes, offset=0):
    reps = lanes // 128
    wide = col if reps == 1 else jnp.concatenate([col] * reps, axis=1)
    ids = (lax.broadcasted_iota(jnp.int32, wide.shape, 1) + offset).astype(jnp.int16)
    return ones_where(wide == ids)


def sum_matrix(row, rows):
    shape = (rows, row.shape[1])
    rows_of = lax.broadcasted_iota(jnp.int32, shape, 0).astype(jnp.int16)
    return ones_where(jnp.broadcast_to(row.astype(jnp.int16), shape) == rows_of)


def kernel(
    fn, fe, es_far, et_far, eb, sr_far, cm_far, ce, cs_far, ct_far, ef, e2, eg_far, nf, n2, ng_far, lw,
    out,
    es, et, sr, cm, cs, ct, eg, ng,
    states, lat, wef, we2, wnf, wn2, wlw, cev,
    a_own, b_tgt, pick, halo, pre, src_col, tgt_col, node_pre, refined,
    part, part_in, col0, col1, choice, choice_in, own, csrc, cs_other, sb, outv,
    load_sem, label_sem, out_sem, halo_ss, halo_rs, part_ss, part_rs, ag_ss, ag_rs, set_ss, set_rs,
):
    s = lax.axis_index("sub")
    d = lax.axis_index("dom")
    subs = NX * NZ * 2
    x = s // (2 * NZ)
    z = lax.rem(s // 2, NZ)
    c = lax.rem(s, 2)
    s_up, s_down = lax.rem(s + 1, subs), lax.rem(s + subs - 1, subs)
    d_up, d_down = lax.rem(d + 1, 4), lax.rem(d + 3, 4)

    def place(xx, zz, cc):
        return xx * (2 * NZ) + zz * 2 + cc

    xs = [lax.rem(x + k, NX) for k in range(NX)]
    dev_z = {k: place(x, lax.rem(z + k + NZ, NZ), c) for k in (1, -1, 2, -2)}
    dev_x = [place(xs[k], z, c) for k in range(NX)]
    sibling = place(x, z, 1 - c)

    barrier = pltpu.get_barrier_semaphore()
    for partner in (s_up, s_down, *dev_z.values(), dev_x[1], dev_x[2], dev_x[3]):
        pl.semaphore_signal(barrier, inc=1, device_id={"sub": partner}, device_id_type=MESH)
    for partner in (d_up, d_down):
        pl.semaphore_signal(barrier, inc=1, device_id={"dom": partner}, device_id_type=MESH)

    labels = [
        pltpu.make_async_copy(a, b, label_sem.at[i])
        for i, (a, b) in enumerate(
            [
                (sr_far, sr), (es_far, es), (et_far, et), (cs_far, cs),
                (cm_far, cm), (ct_far, ct), (eg_far, eg), (ng_far, ng),
            ]
        )
    ]
    pairs = [
        (fn.at[0], states),
        (ef.at[0], wef.at[0]),
        (fe.at[0], lat),
        (e2, we2),
        (nf.at[0], wnf.at[0]),
        (n2, wn2),
        (ce.at[0], cev),
        (ef.at[1], wef.at[1]),
        (nf.at[1], wnf.at[1]),
        (lw, wlw),
    ]
    loads = [pltpu.make_async_copy(a, b, load_sem.at[i]) for i, (a, b) in enumerate(pairs)]
    for copy in loads[:2] + labels + loads[2:]:
        copy.start()

    w = states.shape[1]
    nodes = states.shape[0]
    halo_rows = halo.shape[1]
    coarse = own.shape[0]
    c_edges = cev.shape[0]

    def remote(src, dst, ss, rs, sub=None, dom=None):
        device = {"sub": sub} if dom is None else {"dom": dom}
        return pltpu.make_async_remote_copy(
            src_ref=src, dst_ref=dst, send_sem=ss, recv_sem=rs,
            device_id=device, device_id_type=MESH,
        )

    loads[0].wait()
    loads[1].wait()
    a_own[...] = dot(states[...], wef[0, w : 2 * w]).astype(BF)
    for copy in labels:
        copy.wait()
    listed = jnp.concatenate([column_of(sr[0, k : k + 1, :]) for k in range(4)], axis=0)
    picked = dot(pick_matrix(listed, nodes), a_own[...]).astype(BF)
    pick[...] = picked.reshape(4, halo_rows, w)
    pl.semaphore_wait(barrier, 11)
    halo_copies = [
        remote(pick.at[1], halo.at[0], halo_ss.at[0], halo_rs.at[0], sub=s_up),
        remote(pick.at[0], halo.at[1], halo_ss.at[1], halo_rs.at[1], sub=s_down),
        remote(pick.at[3], halo.at[2], halo_ss.at[2], halo_rs.at[2], dom=d_up),
        remote(pick.at[2], halo.at[3], halo_ss.at[3], halo_rs.at[3], dom=d_down),
    ]
    for copy in halo_copies:
        copy.start()
    cs_copy = remote(cs, cs_other, ag_ss.at[0, 21], ag_rs.at[0, 21], sub=sibling)
    cs_copy.start()

    b_tgt[...] = dot(states[...], wef[0, 2 * w : 3 * w]).astype(BF)
    edges = lat.shape[0]
    src_col[...] = column_of(es[...])
    tgt_col[...] = column_of(et[...])
    loads[2].wait()
    blocks = edges // nodes

    def first(b, carry):
        here = pl.ds(pl.multiple_of(b * nodes, nodes), nodes)
        pre[here, :] = (
            dot(lat[here, :], wef[0, 0:w])
            + dot(pick_matrix(src_col[here, :], nodes), a_own[...])
            + dot(pick_matrix(tgt_col[here, :], nodes), b_tgt[...])
        )
        return carry

    lax.fori_loop(0, blocks, first, 0, unroll=True)
    loads[4].wait()
    node_pre[...] = dot(states[...], wnf[0, 0:w])
    loads[3].wait()
    we2[0] = centred(we2[0])
    loads[5].wait()
    wn2[0] = centred(wn2[0])

    for copy in halo_copies:
        copy.wait()
    exists = (s > 0, s < subs - 1, d > 0, d < 3)
    for k in range(4):
        halo[k] = jnp.where(exists[k], halo[k].astype(F32), 0.0).astype(BF)
    edge_gain = eg[...].astype(F32)
    node_gain = ng[...].astype(F32)
    used = eb[...]

    def second(b, carry):
        start = pl.multiple_of(b * nodes, nodes)
        here = pl.ds(start, nodes)
        table = halo[...].reshape(4 * halo_rows, w)
        v = pre[here, :] + dot(pick_matrix(src_col[here, :], 4 * halo_rows, nodes), table)
        message = scaled(dot(silu(v).astype(BF), we2[0]), edge_gain[0:1])
        lat[here, :] = (lat[here, :].astype(F32) + message).astype(BF)
        return carry

    lax.fori_loop(0, blocks, second, 0, unroll=True)

    block = lax.broadcasted_iota(jnp.int32, (1, edges), 1) // nodes
    targets = jnp.where(block < used, et[...], -1)
    summed = dot(sum_matrix(targets, nodes), lat[...]).astype(BF)
    v = node_pre[...] + dot(summed, wnf[0, w : 2 * w])
    update = scaled(dot(silu(v).astype(BF), wn2[0]), node_gain[0:1])
    refined[...] = (states[...].astype(F32) + update).astype(BF)
    slots = cm[...] - (s - 1) * coarse
    partial = dot(sum_matrix(slots, 3 * coarse), refined[...])
    part[0] = partial[0:coarse].astype(BF)
    part[1] = partial[2 * coarse : 3 * coarse].astype(BF)
    part_copies = [
        remote(part.at[0], part_in.at[0], part_ss.at[0], part_rs.at[0], sub=s_down),
        remote(part.at[1], part_in.at[1], part_ss.at[1], part_rs.at[1], sub=s_up),
    ]
    for copy in part_copies:
        copy.start()
    csrc[0:c_edges, :] = column_of(cs[...])
    cs_copy.wait()
    csrc[c_edges:, :] = column_of(cs_other[...])
    tgt_pick = ones_where(
        column_of(ct[...])[:, 0:coarse]
        == lax.broadcasted_iota(jnp.int32, (c_edges, coarse), 1).astype(jnp.int16)
    )
    tgt_sum = sum_matrix(ct[...], coarse)
    for i in (6, 7, 8, 9):
        loads[i].wait()
    we2[1] = centred(we2[1])
    wn2[1] = centred(wn2[1])
    for copy in part_copies:
        copy.wait()
    own[...] = (
        0.25
        * (
            partial[coarse : 2 * coarse]
            + part_in[0].astype(F32)
            + part_in[1].astype(F32)
        )
    ).astype(BF)

    def gather_parts(g, col):
        ss = lambda i: ag_ss.at[g, i]
        rs = lambda i: ag_rs.at[g, i]

        def send(src, dst, i, target):
            return remote(src, dst, ss(i), rs(i), sub=target)

        def arrived(i, ref):
            remote(ref, ref, ss(i), rs(i), sub=sibling).wait_recv()

        def lines(k, q):
            return col.at[k, GROUPS[q][0] : GROUPS[q][1]]

        def z_send(k, i, step):
            offset = ORDER[i] - step
            to = ORDER.index(offset if offset < 4 else -4)
            return send(col.at[k, i], col.at[k, to], (32 if k else 0) + to, dev_z[step])

        def z_near(k):
            return [z_send(k, 0, step) for step in (2, -2, 1, -1)]

        def z_beyond(k, i):
            if i == 3:
                steps = (1,) if k else (2, 1)
            else:
                steps = (-2, -1) if k else (-1,)
            return [z_send(k, i, step) for step in steps]

        def x_sends(q):
            return [
                send(lines(0, q), lines(3, q), 8 + q, dev_x[1]),
                send(lines(0, q), lines(1, q), 12 + q, dev_x[3]),
            ]

        def x_far():
            return [send(col.at[0, 0], col.at[2, 0], 24, dev_x[2])]

        def choice_send():
            return [send(choice.at[g], choice_in.at[g], 20, sibling)]

        def start(copies):
            for copy in copies:
                copy.start()

        def z_arrived(k, i):
            arrived((32 if k else 0) + i, col.at[k, i])

        def begin():
            start(x_far() + z_near(0) + x_sends(0))

        def forward():
            for i in (3, 4):
                z_arrived(0, i)
                start(z_beyond(0, i))
            arrived(24, col.at[2, 0])
            start(z_near(2))
            for i in (1, 2):
                z_arrived(0, i)
            start(x_sends(1))
            for i in (3, 4):
                z_arrived(2, i)
                start(z_beyond(2, i))
            for i in (5, 6, 7):
                z_arrived(0, i)
            start(x_sends(2))

        def beside():
            for q in range(3):
                arrived(8 + q, lines(3, q))
                arrived(12 + q, lines(1, q))

        def far():
            for i in (1, 2, 5, 6, 7):
                z_arrived(2, i)

        def exchange(theirs):
            choice[g] = theirs
            start(choice_send())

        def exchanged():
            arrived(20, choice_in.at[g])
            return choice_in[g]

        def finish():
            copies = x_far() + choice_send()
            for q in range(3):
                copies += x_sends(q)
            for k in (0, 2):
                copies += z_near(k) + z_beyond(k, 3) + z_beyond(k, 4)
            for copy in copies:
                copy.wait_send()

        return begin, forward, beside, far, exchange, exchanged, finish

    lane = lax.broadcasted_iota(jnp.int32, (1, NZ * coarse), 1)
    turn = lane // coarse
    ahead = jnp.where(lax.rem(turn, 2) == 1, -((turn + 1) // 2), turn // 2)
    span = 2 * coarse
    line_ids = lax.rem(z + ahead + NZ, NZ) * span + c * coarse + lax.rem(lane, coarse)

    finishes = []
    for g, col in enumerate((col0, col1)):
        begin, forward, beside, far, exchange, exchanged, finish = gather_parts(g, col)
        mine = own[...]
        col[0, 0] = mine
        begin()
        picked_own = dot(tgt_pick, mine).astype(BF)
        c_pre = dot(cev[...], wef[1, 0:w]) + dot(picked_own, wef[1, 2 * w : 3 * w])
        n_pre = dot(mine, wnf[1, 0:w])

        def chosen_rows(k, rows):
            labels = jnp.concatenate([csrc[rows, :]] * (NZ * coarse // 128), axis=1)
            return dot(
                ones_where(labels == (line_ids + xs[k] * (NZ * span)).astype(jnp.int16)),
                col[k].reshape(NZ * coarse, w),
            )

        everyone = slice(0, 2 * c_edges)
        forward()
        fetched = chosen_rows(0, everyone)
        beside()
        fetched += chosen_rows(3, everyone) + chosen_rows(1, everyone)
        far()
        exchange((fetched[c_edges:] + chosen_rows(2, slice(c_edges, 2 * c_edges))).astype(BF))
        fetched = fetched[0:c_edges] + chosen_rows(2, slice(0, c_edges))
        fetched += exchanged().astype(F32)
        v = c_pre + dot(fetched.astype(BF), wef[1, w : 2 * w])
        message = scaled(dot(silu(v).astype(BF), we2[1]), edge_gain[1:2])
        new_edges = (cev[...].astype(F32) + message).astype(BF)
        cev[...] = new_edges
        summed = dot(tgt_sum, new_edges).astype(BF)
        v = n_pre + dot(summed, wnf[1, w : 2 * w])
        update = scaled(dot(silu(v).astype(BF), wn2[1]), node_gain[1:2])
        own[...] = (mine.astype(F32) + update).astype(BF)
        finishes.append(finish)

    sb[1] = own[...]
    sb[3] = jnp.zeros_like(sb[3])
    set_copies = [
        remote(sb.at[1], sb.at[0], set_ss.at[0], set_rs.at[0], sub=s_up),
        remote(sb.at[1], sb.at[2], set_ss.at[1], set_rs.at[1], sub=s_down),
    ]
    for copy in set_copies:
        copy.start()
    chosen = pick_matrix(column_of(slots), 4 * coarse)
    for finish in finishes:
        finish()
    for copy in set_copies:
        copy.wait()
    lifted = dot(sb[...].reshape(4 * coarse, w), wlw[...])
    high = lifted.astype(BF)
    low = (lifted - high.astype(F32)).astype(BF)
    halves = []
    for i in range(2):
        rows = slice(i * (nodes // 2), (i + 1) * (nodes // 2))
        outv[rows, :] = (
            refined[rows, :].astype(F32) + dot(chosen[rows], high) + dot(chosen[rows], low)
        ).astype(BF)
        halves.append(pltpu.make_async_copy(outv.at[rows], out.at[0, rows], out_sem.at[i]))
        halves[i].start()
    for copy in halves:
        copy.wait()


def per_device(*arrays):
    fn, fe = arrays[0], arrays[1]
    nodes, w = fn.shape[1], fn.shape[2]
    edges = fe.shape[1]
    halo_rows = arrays[5].shape[2]
    c_edges = arrays[7].shape[1]
    coarse = nodes // 16
    far = pl.BlockSpec(memory_space=pl.ANY)
    near = pl.BlockSpec(memory_space=pltpu.VMEM)
    specs = [near if i == 4 else far for i in range(17)]
    V = pltpu.VMEM
    D = pltpu.SemaphoreType.DMA
    scratch = [
        V((1, edges), jnp.int32),
        V((1, edges), jnp.int32),
        V((1, 4, halo_rows), jnp.int32),
        V((1, nodes), jnp.int32),
        V((1, c_edges), jnp.int32),
        V((1, c_edges), jnp.int32),
        V((2, w), BF),
        V((2, w), BF),
        V((nodes, w), BF),
        V((edges, w), BF),
        V((2, 3 * w, w), BF),
        V((2, w, w), BF),
        V((2, 2 * w, w), BF),
        V((2, w, w), BF),
        V((w, w), BF),
        V((c_edges, w), BF),
        V((nodes, w), BF),
        V((nodes, w), BF),
        V((4, halo_rows, w), BF),
        V((4, halo_rows, w), BF),
        V((edges, w), F32),
        V((edges, 128), jnp.int16),
        V((edges, 128), jnp.int16),
        V((nodes, w), F32),
        V((nodes, w), BF),
        V((2, coarse, w), BF),
        V((2, coarse, w), BF),
        V((NX, NZ, coarse, w), BF),
        V((NX, NZ, coarse, w), BF),
        V((2, c_edges, w), BF),
        V((2, c_edges, w), BF),
        V((coarse, w), BF),
        V((2 * c_edges, 128), jnp.int16),
        V((1, c_edges), jnp.int32),
        V((4, coarse, w), BF),
        V((nodes, w), BF),
        D((10,)),
        D((8,)),
        D((2,)),
        D((4,)),
        D((4,)),
        D((2,)),
        D((2,)),
        D((2, 40)),
        D((2, 40)),
        D((2,)),
        D((2,)),
    ]
    return pl.pallas_call(
        kernel,
        out_shape=jax.ShapeDtypeStruct((1, nodes, w), BF),
        in_specs=specs,
        out_specs=far,
        scratch_shapes=scratch,
        compiler_params=pltpu.CompilerParams(
            collective_id=0, has_side_effects=True, vmem_limit_bytes=56 * 1024 * 1024
        ),
        cost_estimate=pl.CostEstimate(
            flops=9_000_000_000, bytes_accessed=12_000_000, transcendentals=2_000_000
        ),
    )(*arrays)


def solution(mesh):
    row = P("dom", "sub")
    wide = P("dom", "sub", None)
    placed = (
        wide, wide, row, row, row, wide, row, wide, row, row,
        P(), P(), P(), P(), P(), P(), P(),
    )
    return jax.shard_map(
        per_device, mesh=mesh, in_specs=placed, out_specs=wide, check_vma=False
    )
```

```python
import functools

import jax
import jax.numpy as jnp
from jax import lax
from jax.experimental import pallas as pl
from jax.experimental.pallas import tpu as pltpu
from jax.sharding import PartitionSpec as P

EPSILON = 1e-05
BF = jnp.bfloat16
F32 = jnp.float32
MESH = pl.DeviceIdType.MESH
ORDER = (0, -1, 1, -2, 2, -3, 3, -4)
NX, NZ = 4, 8
GROUPS = ((0, 1), (1, 5), (5, 8))


def dot(a, b):
    return jnp.dot(a, b, preferred_element_type=F32)


def silu(v):
    half = 0.5 * v
    return half + half * jnp.tanh(half)


def centred(weight):
    wide = weight.astype(F32)
    return (wide - jnp.mean(wide, axis=-1, keepdims=True)).astype(BF)


def scaled(centre, gain):
    variance = jnp.mean(centre * centre, axis=-1, keepdims=True)
    return centre * lax.rsqrt(variance + EPSILON) * gain


def column_of(row):
    n = row.shape[1]
    parts = [
        jnp.transpose(jnp.broadcast_to(row[:, i : i + 128], (128, 128))) for i in range(0, n, 128)
    ]
    return (parts[0] if len(parts) == 1 else jnp.concatenate(parts, axis=0)).astype(jnp.int16)


def ones_where(mask):
    return jnp.where(mask, jnp.ones((), BF), jnp.zeros((), BF))


def pick_matrix(col, lanes, offset=0):
    reps = lanes // 128
    wide = col if reps == 1 else jnp.concatenate([col] * reps, axis=1)
    ids = (lax.broadcasted_iota(jnp.int32, wide.shape, 1) + offset).astype(jnp.int16)
    return ones_where(wide == ids)


def sum_matrix(row, rows):
    shape = (rows, row.shape[1])
    rows_of = lax.broadcasted_iota(jnp.int32, shape, 0).astype(jnp.int16)
    return ones_where(jnp.broadcast_to(row.astype(jnp.int16), shape) == rows_of)


def kernel(
    fn, fe, es_far, et_far, eb, sr_far, cm_far, ce, cs_far, ct_far, ef, e2, eg_far, nf, n2, ng_far, lw,
    out,
    es, et, sr, cm, cs, ct, eg, ng,
    states, lat, wef, we2, wnf, wn2, wlw, cev,
    a_own, b_tgt, pick, halo, pre, src_col, tgt_col, node_pre, refined,
    part, part_in, col0, col1, choice, choice_in, own, csrc, cs_other, sb, outv,
    load_sem, label_sem, out_sem, halo_ss, halo_rs, part_ss, part_rs, ag_ss, ag_rs, set_ss, set_rs,
):
    s = lax.axis_index("sub")
    d = lax.axis_index("dom")
    subs = NX * NZ * 2
    x = s // (2 * NZ)
    z = lax.rem(s // 2, NZ)
    c = lax.rem(s, 2)
    s_up, s_down = lax.rem(s + 1, subs), lax.rem(s + subs - 1, subs)
    d_up, d_down = lax.rem(d + 1, 4), lax.rem(d + 3, 4)

    def place(xx, zz, cc):
        return xx * (2 * NZ) + zz * 2 + cc

    xs = [lax.rem(x + k, NX) for k in range(NX)]
    dev_z = {k: place(x, lax.rem(z + k + NZ, NZ), c) for k in (1, -1, 2, -2)}
    dev_x = [place(xs[k], z, c) for k in range(NX)]
    sibling = place(x, z, 1 - c)

    barrier = pltpu.get_barrier_semaphore()
    for partner in (s_up, s_down, *dev_z.values(), dev_x[1], dev_x[2], dev_x[3]):
        pl.semaphore_signal(barrier, inc=1, device_id={"sub": partner}, device_id_type=MESH)
    for partner in (d_up, d_down):
        pl.semaphore_signal(barrier, inc=1, device_id={"dom": partner}, device_id_type=MESH)

    labels = [
        pltpu.make_async_copy(a, b, label_sem.at[i])
        for i, (a, b) in enumerate(
            [
                (sr_far, sr), (es_far, es), (et_far, et), (cs_far, cs),
                (cm_far, cm), (ct_far, ct), (eg_far, eg), (ng_far, ng),
            ]
        )
    ]
    w = states.shape[1]
    pairs = [
        (fn.at[0], states),
        (ef.at[0, w : 2 * w], wef.at[0, w : 2 * w]),
        (ef.at[0, 2 * w : 3 * w], wef.at[0, 2 * w : 3 * w]),
        (ef.at[0, 0:w], wef.at[0, 0:w]),
        (fe.at[0], lat),
        (nf.at[0], wnf.at[0]),
        (e2, we2),
        (n2, wn2),
        (ce.at[0], cev),
        (ef.at[1], wef.at[1]),
        (nf.at[1], wnf.at[1]),
        (lw, wlw),
    ]
    loads = [pltpu.make_async_copy(a, b, load_sem.at[i]) for i, (a, b) in enumerate(pairs)]
    for copy in labels[:3] + loads[:2] + labels[3:] + loads[2:]:
        copy.start()

    nodes = states.shape[0]
    halo_rows = halo.shape[1]
    coarse = own.shape[0]
    c_edges = cev.shape[0]

    def remote(src, dst, ss, rs, sub=None, dom=None):
        device = {"sub": sub} if dom is None else {"dom": dom}
        return pltpu.make_async_remote_copy(
            src_ref=src, dst_ref=dst, send_sem=ss, recv_sem=rs,
            device_id=device, device_id_type=MESH,
        )

    for copy in labels[:3]:
        copy.wait()
    listed = jnp.concatenate([column_of(sr[0, k : k + 1, :]) for k in range(4)], axis=0)
    wanted = pick_matrix(listed, nodes)
    tgt_col[...] = column_of(et[...])
    src_col[...] = column_of(es[...])
    loads[0].wait()
    loads[1].wait()
    a_own[...] = dot(states[...], wef[0, w : 2 * w]).astype(BF)
    picked = dot(wanted, a_own[...]).astype(BF)
    pick[...] = picked.reshape(4, halo_rows, w)
    for copy in labels[3:]:
        copy.wait()
    pl.semaphore_wait(barrier, 11)
    halo_copies = [
        remote(pick.at[1], halo.at[0], halo_ss.at[0], halo_rs.at[0], sub=s_up),
        remote(pick.at[0], halo.at[1], halo_ss.at[1], halo_rs.at[1], sub=s_down),
        remote(pick.at[3], halo.at[2], halo_ss.at[2], halo_rs.at[2], dom=d_up),
        remote(pick.at[2], halo.at[3], halo_ss.at[3], halo_rs.at[3], dom=d_down),
    ]
    for copy in halo_copies:
        copy.start()
    cs_copy = remote(cs, cs_other, ag_ss.at[0, 21], ag_rs.at[0, 21], sub=sibling)
    cs_copy.start()

    loads[2].wait()
    b_tgt[...] = dot(states[...], wef[0, 2 * w : 3 * w]).astype(BF)
    edges = lat.shape[0]
    loads[3].wait()
    loads[4].wait()
    blocks = edges // nodes

    def first(b, carry):
        here = pl.ds(pl.multiple_of(b * nodes, nodes), nodes)
        pre[here, :] = (
            dot(lat[here, :], wef[0, 0:w])
            + dot(pick_matrix(src_col[here, :], nodes), a_own[...])
            + dot(pick_matrix(tgt_col[here, :], nodes), b_tgt[...])
        )
        return carry

    lax.fori_loop(0, blocks, first, 0, unroll=True)
    loads[5].wait()
    node_pre[...] = dot(states[...], wnf[0, 0:w])
    loads[6].wait()
    we2[0] = centred(we2[0])
    loads[7].wait()
    wn2[0] = centred(wn2[0])

    for copy in halo_copies:
        copy.wait()
    exists = (s > 0, s < subs - 1, d > 0, d < 3)
    for k in range(4):
        halo[k] = jnp.where(exists[k], halo[k].astype(F32), 0.0).astype(BF)
    edge_gain = eg[...].astype(F32)
    node_gain = ng[...].astype(F32)
    used = eb[...]

    def second(b, carry):
        start = pl.multiple_of(b * nodes, nodes)
        here = pl.ds(start, nodes)
        table = halo[...].reshape(4 * halo_rows, w)
        v = pre[here, :] + dot(pick_matrix(src_col[here, :], 4 * halo_rows, nodes), table)
        message = scaled(dot(silu(v).astype(BF), we2[0]), edge_gain[0:1])
        lat[here, :] = (lat[here, :].astype(F32) + message).astype(BF)
        return carry

    lax.fori_loop(0, blocks, second, 0, unroll=True)

    block = lax.broadcasted_iota(jnp.int32, (1, edges), 1) // nodes
    targets = jnp.where(block < used, et[...], -1)
    summed = dot(sum_matrix(targets, nodes), lat[...]).astype(BF)
    v = node_pre[...] + dot(summed, wnf[0, w : 2 * w])
    update = scaled(dot(silu(v).astype(BF), wn2[0]), node_gain[0:1])
    refined[...] = (states[...].astype(F32) + update).astype(BF)
    slots = cm[...] - (s - 1) * coarse
    partial = dot(sum_matrix(slots, 3 * coarse), refined[...])
    part[0] = partial[0:coarse].astype(BF)
    part[1] = partial[2 * coarse : 3 * coarse].astype(BF)
    part_copies = [
        remote(part.at[0], part_in.at[0], part_ss.at[0], part_rs.at[0], sub=s_down),
        remote(part.at[1], part_in.at[1], part_ss.at[1], part_rs.at[1], sub=s_up),
    ]
    for copy in part_copies:
        copy.start()
    csrc[0:c_edges, :] = column_of(cs[...])
    cs_copy.wait()
    csrc[c_edges:, :] = column_of(cs_other[...])
    tgt_pick = ones_where(
        column_of(ct[...])[:, 0:coarse]
        == lax.broadcasted_iota(jnp.int32, (c_edges, coarse), 1).astype(jnp.int16)
    )
    tgt_sum = sum_matrix(ct[...], coarse)
    for i in (8, 9, 10, 11):
        loads[i].wait()
    we2[1] = centred(we2[1])
    wn2[1] = centred(wn2[1])
    for copy in part_copies:
        copy.wait()
    own[...] = (
        0.25
        * (
            partial[coarse : 2 * coarse]
            + part_in[0].astype(F32)
            + part_in[1].astype(F32)
        )
    ).astype(BF)

    def gather_parts(g, col):
        ss = lambda i: ag_ss.at[g, i]
        rs = lambda i: ag_rs.at[g, i]

        def send(src, dst, i, target):
            return remote(src, dst, ss(i), rs(i), sub=target)

        def arrived(i, ref):
            remote(ref, ref, ss(i), rs(i), sub=sibling).wait_recv()

        def lines(k, q):
            return col.at[k, GROUPS[q][0] : GROUPS[q][1]]

        def z_send(k, i, step):
            offset = ORDER[i] - step
            to = ORDER.index(offset if offset < 4 else -4)
            return send(col.at[k, i], col.at[k, to], (32 if k else 0) + to, dev_z[step])

        def z_near(k):
            return [z_send(k, 0, step) for step in (2, -2, 1, -1)]

        def z_beyond(k, i):
            if i == 3:
                steps = (1,) if k else (2, 1)
            else:
                steps = (-2, -1) if k else (-1,)
            return [z_send(k, i, step) for step in steps]

        def x_sends(q):
            return [
                send(lines(0, q), lines(3, q), 8 + q, dev_x[1]),
                send(lines(0, q), lines(1, q), 12 + q, dev_x[3]),
            ]

        def x_far():
            return [send(col.at[0, 0], col.at[2, 0], 24, dev_x[2])]

        def choice_send():
            return [send(choice.at[g], choice_in.at[g], 20, sibling)]

        def start(copies):
            for copy in copies:
                copy.start()

        def z_arrived(k, i):
            arrived((32 if k else 0) + i, col.at[k, i])

        def begin():
            start(x_far() + z_near(0) + x_sends(0))

        def forward():
            for i in (3, 4):
                z_arrived(0, i)
                start(z_beyond(0, i))
            arrived(24, col.at[2, 0])
            start(z_near(2))
            for i in (1, 2):
                z_arrived(0, i)
            start(x_sends(1))
            for i in (5, 6, 7):
                z_arrived(0, i)
            start(x_sends(2))
            for i in (3, 4):
                z_arrived(2, i)
                start(z_beyond(2, i))

        def beside():
            for q in range(3):
                arrived(8 + q, lines(3, q))
                arrived(12 + q, lines(1, q))

        def far():
            for i in (1, 2, 5, 6, 7):
                z_arrived(2, i)

        def exchange(theirs):
            choice[g] = theirs
            start(choice_send())

        def exchanged():
            arrived(20, choice_in.at[g])
            return choice_in[g]

        def finish():
            copies = x_far() + choice_send()
            for q in range(3):
                copies += x_sends(q)
            for k in (0, 2):
                copies += z_near(k) + z_beyond(k, 3) + z_beyond(k, 4)
            for copy in copies:
                copy.wait_send()

        return begin, forward, beside, far, exchange, exchanged, finish

    lane = lax.broadcasted_iota(jnp.int32, (1, NZ * coarse), 1)
    turn = lane // coarse
    ahead = jnp.where(lax.rem(turn, 2) == 1, -((turn + 1) // 2), turn // 2)
    span = 2 * coarse
    line_ids = lax.rem(z + ahead + NZ, NZ) * span + c * coarse + lax.rem(lane, coarse)

    finishes = []
    for g, col in enumerate((col0, col1)):
        begin, forward, beside, far, exchange, exchanged, finish = gather_parts(g, col)
        mine = own[...]
        col[0, 0] = mine
        begin()
        picked_own = dot(tgt_pick, mine).astype(BF)
        c_pre = dot(cev[...], wef[1, 0:w]) + dot(picked_own, wef[1, 2 * w : 3 * w])
        n_pre = dot(mine, wnf[1, 0:w])

        def chosen_rows(k, rows):
            labels = jnp.concatenate([csrc[rows, :]] * (NZ * coarse // 128), axis=1)
            return dot(
                ones_where(labels == (line_ids + xs[k] * (NZ * span)).astype(jnp.int16)),
                col[k].reshape(NZ * coarse, w),
            )

        everyone = slice(0, 2 * c_edges)
        forward()
        fetched = chosen_rows(0, everyone)
        beside()
        fetched += chosen_rows(3, everyone) + chosen_rows(1, everyone)
        far()
        exchange((fetched[c_edges:] + chosen_rows(2, slice(c_edges, 2 * c_edges))).astype(BF))
        fetched = fetched[0:c_edges] + chosen_rows(2, slice(0, c_edges))
        fetched += exchanged().astype(F32)
        v = c_pre + dot(fetched.astype(BF), wef[1, w : 2 * w])
        message = scaled(dot(silu(v).astype(BF), we2[1]), edge_gain[1:2])
        new_edges = (cev[...].astype(F32) + message).astype(BF)
        cev[...] = new_edges
        summed = dot(tgt_sum, new_edges).astype(BF)
        v = n_pre + dot(summed, wnf[1, w : 2 * w])
        update = scaled(dot(silu(v).astype(BF), wn2[1]), node_gain[1:2])
        own[...] = (mine.astype(F32) + update).astype(BF)
        finishes.append(finish)

    sb[1] = own[...]
    sb[3] = jnp.zeros_like(sb[3])
    set_copies = [
        remote(sb.at[1], sb.at[0], set_ss.at[0], set_rs.at[0], sub=s_up),
        remote(sb.at[1], sb.at[2], set_ss.at[1], set_rs.at[1], sub=s_down),
    ]
    for copy in set_copies:
        copy.start()
    chosen = pick_matrix(column_of(slots), 4 * coarse)
    for finish in finishes:
        finish()
    for copy in set_copies:
        copy.wait()
    lifted = dot(sb[...].reshape(4 * coarse, w), wlw[...])
    high = lifted.astype(BF)
    low = (lifted - high.astype(F32)).astype(BF)
    halves = []
    for i in range(2):
        rows = slice(i * (nodes // 2), (i + 1) * (nodes // 2))
        outv[rows, :] = (
            refined[rows, :].astype(F32) + dot(chosen[rows], high) + dot(chosen[rows], low)
        ).astype(BF)
        halves.append(pltpu.make_async_copy(outv.at[rows], out.at[0, rows], out_sem.at[i]))
        halves[i].start()
    for copy in halves:
        copy.wait()


def per_device(*arrays):
    fn, fe = arrays[0], arrays[1]
    nodes, w = fn.shape[1], fn.shape[2]
    edges = fe.shape[1]
    halo_rows = arrays[5].shape[2]
    c_edges = arrays[7].shape[1]
    coarse = nodes // 16
    far = pl.BlockSpec(memory_space=pl.ANY)
    near = pl.BlockSpec(memory_space=pltpu.VMEM)
    specs = [near if i == 4 else far for i in range(17)]
    V = pltpu.VMEM
    D = pltpu.SemaphoreType.DMA
    scratch = [
        V((1, edges), jnp.int32),
        V((1, edges), jnp.int32),
        V((1, 4, halo_rows), jnp.int32),
        V((1, nodes), jnp.int32),
        V((1, c_edges), jnp.int32),
        V((1, c_edges), jnp.int32),
        V((2, w), BF),
        V((2, w), BF),
        V((nodes, w), BF),
        V((edges, w), BF),
        V((2, 3 * w, w), BF),
        V((2, w, w), BF),
        V((2, 2 * w, w), BF),
        V((2, w, w), BF),
        V((w, w), BF),
        V((c_edges, w), BF),
        V((nodes, w), BF),
        V((nodes, w), BF),
        V((4, halo_rows, w), BF),
        V((4, halo_rows, w), BF),
        V((edges, w), F32),
        V((edges, 128), jnp.int16),
        V((edges, 128), jnp.int16),
        V((nodes, w), F32),
        V((nodes, w), BF),
        V((2, coarse, w), BF),
        V((2, coarse, w), BF),
        V((NX, NZ, coarse, w), BF),
        V((NX, NZ, coarse, w), BF),
        V((2, c_edges, w), BF),
        V((2, c_edges, w), BF),
        V((coarse, w), BF),
        V((2 * c_edges, 128), jnp.int16),
        V((1, c_edges), jnp.int32),
        V((4, coarse, w), BF),
        V((nodes, w), BF),
        D((12,)),
        D((8,)),
        D((2,)),
        D((4,)),
        D((4,)),
        D((2,)),
        D((2,)),
        D((2, 40)),
        D((2, 40)),
        D((2,)),
        D((2,)),
    ]
    return pl.pallas_call(
        kernel,
        out_shape=jax.ShapeDtypeStruct((1, nodes, w), BF),
        in_specs=specs,
        out_specs=far,
        scratch_shapes=scratch,
        compiler_params=pltpu.CompilerParams(
            collective_id=0, has_side_effects=True, vmem_limit_bytes=56 * 1024 * 1024
        ),
        cost_estimate=pl.CostEstimate(
            flops=9_000_000_000, bytes_accessed=12_000_000, transcendentals=2_000_000
        ),
    )(*arrays)


def solution(mesh):
    row = P("dom", "sub")
    wide = P("dom", "sub", None)
    placed = (
        wide, wide, row, row, row, wide, row, wide, row, row,
        P(), P(), P(), P(), P(), P(), P(),
    )
    return jax.shard_map(
        per_device, mesh=mesh, in_specs=placed, out_specs=wide, check_vma=False
    )
```

```python
import functools

import jax
import jax.numpy as jnp
from jax import lax
from jax.experimental import pallas as pl
from jax.experimental.pallas import tpu as pltpu
from jax.sharding import PartitionSpec as P

EPSILON = 1e-05
BF = jnp.bfloat16
F32 = jnp.float32
MESH = pl.DeviceIdType.MESH
ORDER = (0, -1, 1, -2, 2, -3, 3, -4)
NX, NZ = 4, 8
GROUPS = ((0, 1), (1, 5), (5, 8))


def dot(a, b):
    return jnp.dot(a, b, preferred_element_type=F32)


def silu(v):
    half = 0.5 * v
    return half + half * jnp.tanh(half)


def centred(weight):
    wide = weight.astype(F32)
    return (wide - jnp.mean(wide, axis=-1, keepdims=True)).astype(BF)


def scaled(centre, gain):
    variance = jnp.mean(centre * centre, axis=-1, keepdims=True)
    return centre * lax.rsqrt(variance + EPSILON) * gain


def column_of(row):
    n = row.shape[1]
    parts = [
        jnp.transpose(jnp.broadcast_to(row[:, i : i + 128], (128, 128))) for i in range(0, n, 128)
    ]
    return (parts[0] if len(parts) == 1 else jnp.concatenate(parts, axis=0)).astype(jnp.int16)


def ones_where(mask):
    return jnp.where(mask, jnp.ones((), BF), jnp.zeros((), BF))


def pick_matrix(col, lanes, offset=0):
    reps = lanes // 128
    wide = col if reps == 1 else jnp.concatenate([col] * reps, axis=1)
    ids = (lax.broadcasted_iota(jnp.int32, wide.shape, 1) + offset).astype(jnp.int16)
    return ones_where(wide == ids)


def sum_matrix(row, rows):
    shape = (rows, row.shape[1])
    rows_of = lax.broadcasted_iota(jnp.int32, shape, 0).astype(jnp.int16)
    return ones_where(jnp.broadcast_to(row.astype(jnp.int16), shape) == rows_of)


def kernel(
    fn, fe, es_far, et_far, eb, sr_far, cm_far, ce, cs_far, ct_far, ef, e2, eg_far, nf, n2, ng_far, lw,
    out,
    es, et, sr, cm, cs, ct, eg, ng,
    states, lat, wef, we2, wnf, wn2, wlw, cev,
    a_own, b_tgt, pick, halo, pre, src_col, tgt_col, node_pre, refined,
    part, part_in, col0, col1, choice, choice_in, own, csrc, cs_other, wants, sb, outv,
    load_sem, label_sem, out_sem, halo_ss, halo_rs, part_ss, part_rs, ag_ss, ag_rs, set_ss, set_rs,
):
    s = lax.axis_index("sub")
    d = lax.axis_index("dom")
    subs = NX * NZ * 2
    x = s // (2 * NZ)
    z = lax.rem(s // 2, NZ)
    c = lax.rem(s, 2)
    s_up, s_down = lax.rem(s + 1, subs), lax.rem(s + subs - 1, subs)
    d_up, d_down = lax.rem(d + 1, 4), lax.rem(d + 3, 4)

    def place(xx, zz, cc):
        return xx * (2 * NZ) + zz * 2 + cc

    xs = [lax.rem(x + k, NX) for k in range(NX)]
    dev_z = {k: place(x, lax.rem(z + k + NZ, NZ), c) for k in (1, -1, 2, -2)}
    dev_x = [place(xs[k], z, c) for k in range(NX)]
    sibling = place(x, z, 1 - c)

    barrier = pltpu.get_barrier_semaphore()
    for partner in (s_up, s_down, *dev_z.values(), dev_x[1], dev_x[2], dev_x[3]):
        pl.semaphore_signal(barrier, inc=1, device_id={"sub": partner}, device_id_type=MESH)
    for partner in (d_up, d_down):
        pl.semaphore_signal(barrier, inc=1, device_id={"dom": partner}, device_id_type=MESH)

    labels = [
        pltpu.make_async_copy(a, b, label_sem.at[i])
        for i, (a, b) in enumerate(
            [
                (sr_far, sr), (es_far, es), (et_far, et), (cs_far, cs),
                (cm_far, cm), (ct_far, ct), (eg_far, eg), (ng_far, ng),
            ]
        )
    ]
    w = states.shape[1]
    pairs = [
        (fn.at[0], states),
        (ef.at[0, w : 2 * w], wef.at[0, w : 2 * w]),
        (ef.at[0, 2 * w : 3 * w], wef.at[0, 2 * w : 3 * w]),
        (ef.at[0, 0:w], wef.at[0, 0:w]),
        (fe.at[0], lat),
        (nf.at[0], wnf.at[0]),
        (e2, we2),
        (n2, wn2),
        (ce.at[0], cev),
        (ef.at[1], wef.at[1]),
        (nf.at[1], wnf.at[1]),
        (lw, wlw),
    ]
    loads = [pltpu.make_async_copy(a, b, load_sem.at[i]) for i, (a, b) in enumerate(pairs)]
    for copy in labels[:3] + loads[:2] + labels[3:] + loads[2:]:
        copy.start()

    nodes = states.shape[0]
    halo_rows = halo.shape[1]
    coarse = own.shape[0]
    c_edges = cev.shape[0]

    def remote(src, dst, ss, rs, sub=None, dom=None):
        device = {"sub": sub} if dom is None else {"dom": dom}
        return pltpu.make_async_remote_copy(
            src_ref=src, dst_ref=dst, send_sem=ss, recv_sem=rs,
            device_id=device, device_id_type=MESH,
        )

    for copy in labels[:3]:
        copy.wait()
    listed = jnp.concatenate([column_of(sr[0, k : k + 1, :]) for k in range(4)], axis=0)
    wanted = pick_matrix(listed, nodes)
    tgt_col[...] = column_of(et[...])
    src_col[...] = column_of(es[...])
    loads[0].wait()
    loads[1].wait()
    a_own[...] = dot(states[...], wef[0, w : 2 * w]).astype(BF)
    picked = dot(wanted, a_own[...]).astype(BF)
    pick[...] = picked.reshape(4, halo_rows, w)
    for copy in labels[3:]:
        copy.wait()
    pl.semaphore_wait(barrier, 11)
    halo_copies = [
        remote(pick.at[1], halo.at[0], halo_ss.at[0], halo_rs.at[0], sub=s_up),
        remote(pick.at[0], halo.at[1], halo_ss.at[1], halo_rs.at[1], sub=s_down),
        remote(pick.at[3], halo.at[2], halo_ss.at[2], halo_rs.at[2], dom=d_up),
        remote(pick.at[2], halo.at[3], halo_ss.at[3], halo_rs.at[3], dom=d_down),
    ]
    for copy in halo_copies:
        copy.start()
    cs_copy = remote(cs, cs_other, ag_ss.at[0, 21], ag_rs.at[0, 21], sub=sibling)
    cs_copy.start()

    loads[2].wait()
    b_tgt[...] = dot(states[...], wef[0, 2 * w : 3 * w]).astype(BF)
    edges = lat.shape[0]
    loads[3].wait()
    loads[4].wait()
    blocks = edges // nodes

    def first(b, carry):
        here = pl.ds(pl.multiple_of(b * nodes, nodes), nodes)
        pre[here, :] = (
            dot(lat[here, :], wef[0, 0:w])
            + dot(pick_matrix(src_col[here, :], nodes), a_own[...])
            + dot(pick_matrix(tgt_col[here, :], nodes), b_tgt[...])
        )
        return carry

    lax.fori_loop(0, blocks, first, 0, unroll=True)
    loads[5].wait()
    node_pre[...] = dot(states[...], wnf[0, 0:w])
    loads[6].wait()
    we2[0] = centred(we2[0])
    loads[7].wait()
    wn2[0] = centred(wn2[0])

    for copy in halo_copies:
        copy.wait()
    exists = (s > 0, s < subs - 1, d > 0, d < 3)
    for k in range(4):
        halo[k] = jnp.where(exists[k], halo[k].astype(F32), 0.0).astype(BF)
    edge_gain = eg[...].astype(F32)
    node_gain = ng[...].astype(F32)
    used = eb[...]

    def second(b, carry):
        start = pl.multiple_of(b * nodes, nodes)
        here = pl.ds(start, nodes)
        table = halo[...].reshape(4 * halo_rows, w)
        v = pre[here, :] + dot(pick_matrix(src_col[here, :], 4 * halo_rows, nodes), table)
        message = scaled(dot(silu(v).astype(BF), we2[0]), edge_gain[0:1])
        lat[here, :] = (lat[here, :].astype(F32) + message).astype(BF)
        return carry

    lax.fori_loop(0, blocks, second, 0, unroll=True)

    block = lax.broadcasted_iota(jnp.int32, (1, edges), 1) // nodes
    targets = jnp.where(block < used, et[...], -1)
    summed = dot(sum_matrix(targets, nodes), lat[...]).astype(BF)
    v = node_pre[...] + dot(summed, wnf[0, w : 2 * w])
    update = scaled(dot(silu(v).astype(BF), wn2[0]), node_gain[0:1])
    refined[...] = (states[...].astype(F32) + update).astype(BF)
    slots = cm[...] - (s - 1) * coarse
    partial = dot(sum_matrix(slots, 3 * coarse), refined[...])
    part[0] = partial[0:coarse].astype(BF)
    part[1] = partial[2 * coarse : 3 * coarse].astype(BF)
    part_copies = [
        remote(part.at[0], part_in.at[0], part_ss.at[0], part_rs.at[0], sub=s_down),
        remote(part.at[1], part_in.at[1], part_ss.at[1], part_rs.at[1], sub=s_up),
    ]
    for copy in part_copies:
        copy.start()
    csrc[0:c_edges, :] = column_of(cs[...])
    cs_copy.wait()
    csrc[c_edges:, :] = column_of(cs_other[...])
    tgt_pick = ones_where(
        column_of(ct[...])[:, 0:coarse]
        == lax.broadcasted_iota(jnp.int32, (c_edges, coarse), 1).astype(jnp.int16)
    )
    tgt_sum = sum_matrix(ct[...], coarse)
    for i in (8, 9, 10, 11):
        loads[i].wait()
    for copy in part_copies:
        copy.wait()
    own[...] = (
        0.25
        * (
            partial[coarse : 2 * coarse]
            + part_in[0].astype(F32)
            + part_in[1].astype(F32)
        )
    ).astype(BF)

    def gather_parts(g, col):
        ss = lambda i: ag_ss.at[g, i]
        rs = lambda i: ag_rs.at[g, i]

        def send(src, dst, i, target):
            return remote(src, dst, ss(i), rs(i), sub=target)

        def arrived(i, ref):
            remote(ref, ref, ss(i), rs(i), sub=sibling).wait_recv()

        def lines(k, q):
            return col.at[k, GROUPS[q][0] : GROUPS[q][1]]

        def z_send(k, i, step):
            offset = ORDER[i] - step
            to = ORDER.index(offset if offset < 4 else -4)
            return send(col.at[k, i], col.at[k, to], (32 if k else 0) + to, dev_z[step])

        def z_near(k):
            return [z_send(k, 0, step) for step in (2, -2, 1, -1)]

        def z_beyond(k, i):
            if i == 3:
                steps = (1,) if k else (2, 1)
            else:
                steps = (-2, -1) if k else (-1,)
            return [z_send(k, i, step) for step in steps]

        def x_sends(q):
            return [
                send(lines(0, q), lines(3, q), 8 + q, dev_x[1]),
                send(lines(0, q), lines(1, q), 12 + q, dev_x[3]),
            ]

        def x_far():
            return [send(col.at[0, 0], col.at[2, 0], 24, dev_x[2])]

        def choice_send():
            return [send(choice.at[g], choice_in.at[g], 20, sibling)]

        def start(copies):
            for copy in copies:
                copy.start()

        def z_arrived(k, i):
            arrived((32 if k else 0) + i, col.at[k, i])

        def begin():
            start(x_far() + z_near(0) + x_sends(0))

        def forward():
            for i in (3, 4):
                z_arrived(0, i)
                start(z_beyond(0, i))
            arrived(24, col.at[2, 0])
            start(z_near(2))
            for i in (1, 2):
                z_arrived(0, i)
            start(x_sends(1))
            for i in (5, 6, 7):
                z_arrived(0, i)
            start(x_sends(2))
            for i in (3, 4):
                z_arrived(2, i)
                start(z_beyond(2, i))

        def beside():
            for q in range(3):
                arrived(8 + q, lines(3, q))
                arrived(12 + q, lines(1, q))

        def far():
            for i in (1, 2, 5, 6, 7):
                z_arrived(2, i)

        def exchange(theirs):
            choice[g] = theirs
            start(choice_send())

        def exchanged():
            arrived(20, choice_in.at[g])
            return choice_in[g]

        def finish():
            copies = x_far() + choice_send()
            for q in range(3):
                copies += x_sends(q)
            for k in (0, 2):
                copies += z_near(k) + z_beyond(k, 3) + z_beyond(k, 4)
            for copy in copies:
                copy.wait_send()

        return begin, forward, beside, far, exchange, exchanged, finish

    lane = lax.broadcasted_iota(jnp.int32, (1, NZ * coarse), 1)
    turn = lane // coarse
    ahead = jnp.where(lax.rem(turn, 2) == 1, -((turn + 1) // 2), turn // 2)
    span = 2 * coarse
    plane = NZ * coarse
    line_ids = lax.rem(z + ahead + NZ, NZ) * span + c * coarse + lax.rem(lane, coarse)

    finishes = []
    for g, col in enumerate((col0, col1)):
        begin, forward, beside, far, exchange, exchanged, finish = gather_parts(g, col)
        mine = own[...]
        col[0, 0] = mine
        begin()
        picked_own = dot(tgt_pick, mine).astype(BF)
        c_pre = dot(cev[...], wef[1, 0:w]) + dot(picked_own, wef[1, 2 * w : 3 * w])
        n_pre = dot(mine, wnf[1, 0:w])

        forward()
        if g == 0:
            we2[1] = centred(we2[1])
            wn2[1] = centred(wn2[1])
            labels = jnp.concatenate([csrc[...]] * (plane // 128), axis=1)
            for k in range(NX):
                ids = (line_ids + xs[k] * (NZ * span)).astype(jnp.int16)
                wants[:, k * plane : (k + 1) * plane] = ones_where(labels == ids)
        fetched = dot(wants[:, 0:plane], col[0].reshape(plane, w))
        beside()
        far()
        others = col[1:NX].reshape((NX - 1) * plane, w)
        exchange((fetched[c_edges:] + dot(wants[c_edges:, plane:], others)).astype(BF))
        fetched = (fetched[0:c_edges] + dot(wants[0:c_edges, plane:], others)).astype(BF)
        c_pre += dot(fetched, wef[1, w : 2 * w])
        v = c_pre + dot(exchanged(), wef[1, w : 2 * w])
        message = scaled(dot(silu(v).astype(BF), we2[1]), edge_gain[1:2])
        new_edges = (cev[...].astype(F32) + message).astype(BF)
        cev[...] = new_edges
        summed = dot(tgt_sum, new_edges).astype(BF)
        v = n_pre + dot(summed, wnf[1, w : 2 * w])
        update = scaled(dot(silu(v).astype(BF), wn2[1]), node_gain[1:2])
        own[...] = (mine.astype(F32) + update).astype(BF)
        finishes.append(finish)

    sb[1] = own[...]
    sb[3] = jnp.zeros_like(sb[3])
    set_copies = [
        remote(sb.at[1], sb.at[0], set_ss.at[0], set_rs.at[0], sub=s_up),
        remote(sb.at[1], sb.at[2], set_ss.at[1], set_rs.at[1], sub=s_down),
    ]
    for copy in set_copies:
        copy.start()
    chosen = pick_matrix(column_of(slots), 4 * coarse)
    for finish in finishes:
        finish()
    for copy in set_copies:
        copy.wait()
    lifted = dot(sb[...].reshape(4 * coarse, w), wlw[...])
    high = lifted.astype(BF)
    low = (lifted - high.astype(F32)).astype(BF)
    halves = []
    for i in range(2):
        rows = slice(i * (nodes // 2), (i + 1) * (nodes // 2))
        outv[rows, :] = (
            refined[rows, :].astype(F32) + dot(chosen[rows], high) + dot(chosen[rows], low)
        ).astype(BF)
        halves.append(pltpu.make_async_copy(outv.at[rows], out.at[0, rows], out_sem.at[i]))
        halves[i].start()
    for copy in halves:
        copy.wait()


def per_device(*arrays):
    fn, fe = arrays[0], arrays[1]
    nodes, w = fn.shape[1], fn.shape[2]
    edges = fe.shape[1]
    halo_rows = arrays[5].shape[2]
    c_edges = arrays[7].shape[1]
    coarse = nodes // 16
    far = pl.BlockSpec(memory_space=pl.ANY)
    near = pl.BlockSpec(memory_space=pltpu.VMEM)
    specs = [near if i == 4 else far for i in range(17)]
    V = pltpu.VMEM
    D = pltpu.SemaphoreType.DMA
    scratch = [
        V((1, edges), jnp.int32),
        V((1, edges), jnp.int32),
        V((1, 4, halo_rows), jnp.int32),
        V((1, nodes), jnp.int32),
        V((1, c_edges), jnp.int32),
        V((1, c_edges), jnp.int32),
        V((2, w), BF),
        V((2, w), BF),
        V((nodes, w), BF),
        V((edges, w), BF),
        V((2, 3 * w, w), BF),
        V((2, w, w), BF),
        V((2, 2 * w, w), BF),
        V((2, w, w), BF),
        V((w, w), BF),
        V((c_edges, w), BF),
        V((nodes, w), BF),
        V((nodes, w), BF),
        V((4, halo_rows, w), BF),
        V((4, halo_rows, w), BF),
        V((edges, w), F32),
        V((edges, 128), jnp.int16),
        V((edges, 128), jnp.int16),
        V((nodes, w), F32),
        V((nodes, w), BF),
        V((2, coarse, w), BF),
        V((2, coarse, w), BF),
        V((NX, NZ, coarse, w), BF),
        V((NX, NZ, coarse, w), BF),
        V((2, c_edges, w), BF),
        V((2, c_edges, w), BF),
        V((coarse, w), BF),
        V((2 * c_edges, 128), jnp.int16),
        V((1, c_edges), jnp.int32),
        V((2 * c_edges, NX * NZ * coarse), BF),
        V((4, coarse, w), BF),
        V((nodes, w), BF),
        D((12,)),
        D((8,)),
        D((2,)),
        D((4,)),
        D((4,)),
        D((2,)),
        D((2,)),
        D((2, 40)),
        D((2, 40)),
        D((2,)),
        D((2,)),
    ]
    return pl.pallas_call(
        kernel,
        out_shape=jax.ShapeDtypeStruct((1, nodes, w), BF),
        in_specs=specs,
        out_specs=far,
        scratch_shapes=scratch,
        compiler_params=pltpu.CompilerParams(
            collective_id=0, has_side_effects=True, vmem_limit_bytes=56 * 1024 * 1024
        ),
        cost_estimate=pl.CostEstimate(
            flops=9_000_000_000, bytes_accessed=12_000_000, transcendentals=2_000_000
        ),
    )(*arrays)


def solution(mesh):
    row = P("dom", "sub")
    wide = P("dom", "sub", None)
    placed = (
        wide, wide, row, row, row, wide, row, wide, row, row,
        P(), P(), P(), P(), P(), P(), P(),
    )
    return jax.shard_map(
        per_device, mesh=mesh, in_specs=placed, out_specs=wide, check_vma=False
    )
```

```python
import functools

import jax
import jax.numpy as jnp
from jax import lax
from jax.experimental import pallas as pl
from jax.experimental.pallas import tpu as pltpu
from jax.sharding import PartitionSpec as P

EPSILON = 1e-05
BF = jnp.bfloat16
F32 = jnp.float32
MESH = pl.DeviceIdType.MESH
ORDER = (0, -1, 1, -2, 2, -3, 3, -4)
NX, NZ = 4, 8
GROUPS = ((0, 1), (1, 5), (5, 8))


def dot(a, b):
    return jnp.dot(a, b, preferred_element_type=F32)


def silu(v):
    half = 0.5 * v
    return half + half * jnp.tanh(half)


def centred(weight):
    wide = weight.astype(F32)
    return (wide - jnp.mean(wide, axis=-1, keepdims=True)).astype(BF)


def scaled(centre, gain):
    variance = jnp.mean(centre * centre, axis=-1, keepdims=True)
    return centre * lax.rsqrt(variance + EPSILON) * gain


def column_of(row):
    n = row.shape[1]
    parts = [
        jnp.transpose(jnp.broadcast_to(row[:, i : i + 128], (128, 128))) for i in range(0, n, 128)
    ]
    return (parts[0] if len(parts) == 1 else jnp.concatenate(parts, axis=0)).astype(jnp.int16)


def ones_where(mask):
    return jnp.where(mask, jnp.ones((), BF), jnp.zeros((), BF))


def pick_matrix(col, lanes, offset=0):
    reps = lanes // 128
    wide = col if reps == 1 else jnp.concatenate([col] * reps, axis=1)
    ids = (lax.broadcasted_iota(jnp.int32, wide.shape, 1) + offset).astype(jnp.int16)
    return ones_where(wide == ids)


def sum_matrix(row, rows):
    shape = (rows, row.shape[1])
    rows_of = lax.broadcasted_iota(jnp.int32, shape, 0).astype(jnp.int16)
    return ones_where(jnp.broadcast_to(row.astype(jnp.int16), shape) == rows_of)


def kernel(
    fn, fe, es_far, et_far, eb, sr_far, cm_far, ce, cs_far, ct_far, ef, e2, eg_far, nf, n2, ng_far, lw,
    out,
    es, et, sr, cm, cs, ct, eg, ng,
    states, lat, wef, we2, wnf, wn2, wlw, cev,
    a_own, b_tgt, pick, halo, pre, src_col, tgt_col, node_pre, refined,
    part, part_in, col0, col1, choice, choice_in, own, csrc, cs_other, wants, sb, outv,
    load_sem, label_sem, out_sem, halo_ss, halo_rs, part_ss, part_rs, ag_ss, ag_rs, set_ss, set_rs,
):
    s = lax.axis_index("sub")
    d = lax.axis_index("dom")
    subs = NX * NZ * 2
    x = s // (2 * NZ)
    z = lax.rem(s // 2, NZ)
    c = lax.rem(s, 2)
    s_up, s_down = lax.rem(s + 1, subs), lax.rem(s + subs - 1, subs)
    d_up, d_down = lax.rem(d + 1, 4), lax.rem(d + 3, 4)

    def place(xx, zz, cc):
        return xx * (2 * NZ) + zz * 2 + cc

    xs = [lax.rem(x + k, NX) for k in range(NX)]
    dev_z = {k: place(x, lax.rem(z + k + NZ, NZ), c) for k in (1, -1, 2, -2)}
    dev_x = [place(xs[k], z, c) for k in range(NX)]
    sibling = place(x, z, 1 - c)

    barrier = pltpu.get_barrier_semaphore()
    for partner in (s_up, s_down, *dev_z.values(), dev_x[1], dev_x[2], dev_x[3]):
        pl.semaphore_signal(barrier, inc=1, device_id={"sub": partner}, device_id_type=MESH)
    for partner in (d_up, d_down):
        pl.semaphore_signal(barrier, inc=1, device_id={"dom": partner}, device_id_type=MESH)

    labels = [
        pltpu.make_async_copy(a, b, label_sem.at[i])
        for i, (a, b) in enumerate(
            [
                (sr_far, sr), (es_far, es), (et_far, et), (cs_far, cs),
                (cm_far, cm), (ct_far, ct), (eg_far, eg), (ng_far, ng),
            ]
        )
    ]
    w = states.shape[1]
    pairs = [
        (fn.at[0], states),
        (ef.at[0, w : 2 * w], wef.at[0, w : 2 * w]),
        (ef.at[0, 2 * w : 3 * w], wef.at[0, 2 * w : 3 * w]),
        (ef.at[0, 0:w], wef.at[0, 0:w]),
        (fe.at[0], lat),
        (nf.at[0], wnf.at[0]),
        (e2, we2),
        (n2, wn2),
        (ce.at[0], cev),
        (ef.at[1], wef.at[1]),
        (nf.at[1], wnf.at[1]),
        (lw, wlw),
    ]
    loads = [pltpu.make_async_copy(a, b, load_sem.at[i]) for i, (a, b) in enumerate(pairs)]
    for copy in labels[:3] + loads[:2] + labels[3:] + loads[2:]:
        copy.start()

    nodes = states.shape[0]
    halo_rows = halo.shape[1]
    coarse = own.shape[0]
    c_edges = cev.shape[0]

    def remote(src, dst, ss, rs, sub=None, dom=None):
        device = {"sub": sub} if dom is None else {"dom": dom}
        return pltpu.make_async_remote_copy(
            src_ref=src, dst_ref=dst, send_sem=ss, recv_sem=rs,
            device_id=device, device_id_type=MESH,
        )

    for copy in labels[:3]:
        copy.wait()
    listed = jnp.concatenate([column_of(sr[0, k : k + 1, :]) for k in range(4)], axis=0)
    wanted = pick_matrix(listed, nodes)
    tgt_col[...] = column_of(et[...])
    loads[0].wait()
    loads[1].wait()
    a_own[...] = dot(states[...], wef[0, w : 2 * w]).astype(BF)
    picked = dot(wanted, a_own[...]).astype(BF)
    pick[...] = picked.reshape(4, halo_rows, w)
    for copy in labels[3:]:
        copy.wait()
    pl.semaphore_wait(barrier, 11)
    halo_copies = [
        remote(pick.at[1], halo.at[0], halo_ss.at[0], halo_rs.at[0], sub=s_up),
        remote(pick.at[0], halo.at[1], halo_ss.at[1], halo_rs.at[1], sub=s_down),
        remote(pick.at[3], halo.at[2], halo_ss.at[2], halo_rs.at[2], dom=d_up),
        remote(pick.at[2], halo.at[3], halo_ss.at[3], halo_rs.at[3], dom=d_down),
    ]
    for copy in halo_copies:
        copy.start()
    cs_copy = remote(cs, cs_other, ag_ss.at[0, 21], ag_rs.at[0, 21], sub=sibling)
    cs_copy.start()

    src_col[...] = column_of(es[...])
    loads[2].wait()
    b_tgt[...] = dot(states[...], wef[0, 2 * w : 3 * w]).astype(BF)
    edges = lat.shape[0]
    loads[3].wait()
    loads[4].wait()
    blocks = edges // nodes

    def first(b, carry):
        here = pl.ds(pl.multiple_of(b * nodes, nodes), nodes)
        pre[here, :] = (
            dot(lat[here, :], wef[0, 0:w])
            + dot(pick_matrix(src_col[here, :], nodes), a_own[...])
            + dot(pick_matrix(tgt_col[here, :], nodes), b_tgt[...])
        )
        return carry

    lax.fori_loop(0, blocks, first, 0, unroll=True)
    loads[5].wait()
    node_pre[...] = dot(states[...], wnf[0, 0:w])
    loads[6].wait()
    we2[0] = centred(we2[0])
    loads[7].wait()
    wn2[0] = centred(wn2[0])

    for copy in halo_copies:
        copy.wait()
    exists = (s > 0, s < subs - 1, d > 0, d < 3)
    for k in range(4):
        halo[k] = jnp.where(exists[k], halo[k].astype(F32), 0.0).astype(BF)
    edge_gain = eg[...].astype(F32)
    node_gain = ng[...].astype(F32)
    used = eb[...]

    def second(b, carry):
        start = pl.multiple_of(b * nodes, nodes)
        here = pl.ds(start, nodes)
        table = halo[...].reshape(4 * halo_rows, w)
        v = pre[here, :] + dot(pick_matrix(src_col[here, :], 4 * halo_rows, nodes), table)
        message = scaled(dot(silu(v).astype(BF), we2[0]), edge_gain[0:1])
        lat[here, :] = (lat[here, :].astype(F32) + message).astype(BF)
        return carry

    lax.fori_loop(0, blocks, second, 0, unroll=True)

    block = lax.broadcasted_iota(jnp.int32, (1, edges), 1) // nodes
    targets = jnp.where(block < used, et[...], -1)
    summed = dot(sum_matrix(targets, nodes), lat[...]).astype(BF)
    v = node_pre[...] + dot(summed, wnf[0, w : 2 * w])
    update = scaled(dot(silu(v).astype(BF), wn2[0]), node_gain[0:1])
    refined[...] = (states[...].astype(F32) + update).astype(BF)
    slots = cm[...] - (s - 1) * coarse
    partial = dot(sum_matrix(slots, 3 * coarse), refined[...])
    part[0] = partial[0:coarse].astype(BF)
    part[1] = partial[2 * coarse : 3 * coarse].astype(BF)
    part_copies = [
        remote(part.at[0], part_in.at[0], part_ss.at[0], part_rs.at[0], sub=s_down),
        remote(part.at[1], part_in.at[1], part_ss.at[1], part_rs.at[1], sub=s_up),
    ]
    for copy in part_copies:
        copy.start()
    csrc[0:c_edges, :] = column_of(cs[...])
    cs_copy.wait()
    csrc[c_edges:, :] = column_of(cs_other[...])
    tgt_pick = ones_where(
        column_of(ct[...])[:, 0:coarse]
        == lax.broadcasted_iota(jnp.int32, (c_edges, coarse), 1).astype(jnp.int16)
    )
    tgt_sum = sum_matrix(ct[...], coarse)
    for i in (8, 9, 10, 11):
        loads[i].wait()
    for copy in part_copies:
        copy.wait()
    own[...] = (
        0.25
        * (
            partial[coarse : 2 * coarse]
            + part_in[0].astype(F32)
            + part_in[1].astype(F32)
        )
    ).astype(BF)

    def gather_parts(g, col):
        ss = lambda i: ag_ss.at[g, i]
        rs = lambda i: ag_rs.at[g, i]

        def send(src, dst, i, target):
            return remote(src, dst, ss(i), rs(i), sub=target)

        def arrived(i, ref):
            remote(ref, ref, ss(i), rs(i), sub=sibling).wait_recv()

        def lines(k, q):
            return col.at[k, GROUPS[q][0] : GROUPS[q][1]]

        def z_send(k, i, step):
            offset = ORDER[i] - step
            to = ORDER.index(offset if offset < 4 else -4)
            return send(col.at[k, i], col.at[k, to], (32 if k else 0) + to, dev_z[step])

        def z_near(k, steps=(2, -2, 1, -1)):
            return [z_send(k, 0, step) for step in steps]

        def z_beyond(k, i):
            if i == 3:
                steps = (1,) if k else (2, 1)
            else:
                steps = (-2, -1) if k else (-1,)
            return [z_send(k, i, step) for step in steps]

        def x_sends(q):
            return [
                send(lines(0, q), lines(3, q), 8 + q, dev_x[1]),
                send(lines(0, q), lines(1, q), 12 + q, dev_x[3]),
            ]

        def x_far():
            return [send(col.at[0, 0], col.at[2, 0], 24, dev_x[2])]

        def choice_send():
            return [send(choice.at[g], choice_in.at[g], 20, sibling)]

        def start(copies):
            for copy in copies:
                copy.start()

        def z_arrived(k, i):
            arrived((32 if k else 0) + i, col.at[k, i])

        def begin():
            start(x_far() + z_near(0) + x_sends(0))

        def forward():
            arrived(24, col.at[2, 0])
            start(z_near(2, (2, -2)))
            for i in (3, 4):
                z_arrived(0, i)
                start(z_beyond(0, i))
            for i in (1, 2):
                z_arrived(0, i)
            start(x_sends(1))
            start(z_near(2, (1, -1)))
            for i in (5, 6, 7):
                z_arrived(0, i)
            start(x_sends(2))
            for i in (3, 4):
                z_arrived(2, i)
                start(z_beyond(2, i))

        def beside():
            for q in range(3):
                arrived(8 + q, lines(3, q))
                arrived(12 + q, lines(1, q))

        def far():
            for i in (1, 2, 5, 6, 7):
                z_arrived(2, i)

        def exchange(theirs):
            choice[g] = theirs
            start(choice_send())

        def exchanged():
            arrived(20, choice_in.at[g])
            return choice_in[g]

        def finish():
            copies = x_far() + choice_send()
            for q in range(3):
                copies += x_sends(q)
            for k in (0, 2):
                copies += z_near(k) + z_beyond(k, 3) + z_beyond(k, 4)
            for copy in copies:
                copy.wait_send()

        return begin, forward, beside, far, exchange, exchanged, finish

    lane = lax.broadcasted_iota(jnp.int32, (1, NZ * coarse), 1)
    turn = lane // coarse
    ahead = jnp.where(lax.rem(turn, 2) == 1, -((turn + 1) // 2), turn // 2)
    span = 2 * coarse
    plane = NZ * coarse
    line_ids = lax.rem(z + ahead + NZ, NZ) * span + c * coarse + lax.rem(lane, coarse)

    finishes = []
    for g, col in enumerate((col0, col1)):
        begin, forward, beside, far, exchange, exchanged, finish = gather_parts(g, col)
        mine = own[...]
        col[0, 0] = mine
        begin()
        picked_own = dot(tgt_pick, mine).astype(BF)
        c_pre = dot(cev[...], wef[1, 0:w]) + dot(picked_own, wef[1, 2 * w : 3 * w])
        n_pre = dot(mine, wnf[1, 0:w])

        forward()
        if g == 0:
            we2[1] = centred(we2[1])
            wn2[1] = centred(wn2[1])
            labels = jnp.concatenate([csrc[...]] * (plane // 128), axis=1)
            for k in range(NX):
                ids = (line_ids + xs[k] * (NZ * span)).astype(jnp.int16)
                wants[:, k * plane : (k + 1) * plane] = ones_where(labels == ids)
        fetched = dot(wants[:, 0:plane], col[0].reshape(plane, w))
        beside()
        far()
        others = col[1:NX].reshape((NX - 1) * plane, w)
        exchange((fetched[c_edges:] + dot(wants[c_edges:, plane:], others)).astype(BF))
        fetched = (fetched[0:c_edges] + dot(wants[0:c_edges, plane:], others)).astype(BF)
        c_pre += dot(fetched, wef[1, w : 2 * w])
        v = c_pre + dot(exchanged(), wef[1, w : 2 * w])
        message = scaled(dot(silu(v).astype(BF), we2[1]), edge_gain[1:2])
        new_edges = (cev[...].astype(F32) + message).astype(BF)
        cev[...] = new_edges
        summed = dot(tgt_sum, new_edges).astype(BF)
        v = n_pre + dot(summed, wnf[1, w : 2 * w])
        update = scaled(dot(silu(v).astype(BF), wn2[1]), node_gain[1:2])
        own[...] = (mine.astype(F32) + update).astype(BF)
        finishes.append(finish)

    sb[1] = own[...]
    sb[3] = jnp.zeros_like(sb[3])
    set_copies = [
        remote(sb.at[1], sb.at[0], set_ss.at[0], set_rs.at[0], sub=s_up),
        remote(sb.at[1], sb.at[2], set_ss.at[1], set_rs.at[1], sub=s_down),
    ]
    for copy in set_copies:
        copy.start()
    chosen = pick_matrix(column_of(slots), 4 * coarse)
    for finish in finishes:
        finish()
    for copy in set_copies:
        copy.wait()
    lifted = dot(sb[...].reshape(4 * coarse, w), wlw[...])
    high = lifted.astype(BF)
    low = (lifted - high.astype(F32)).astype(BF)
    halves = []
    for i in range(2):
        rows = slice(i * (nodes // 2), (i + 1) * (nodes // 2))
        outv[rows, :] = (
            refined[rows, :].astype(F32) + dot(chosen[rows], high) + dot(chosen[rows], low)
        ).astype(BF)
        halves.append(pltpu.make_async_copy(outv.at[rows], out.at[0, rows], out_sem.at[i]))
        halves[i].start()
    for copy in halves:
        copy.wait()


def per_device(*arrays):
    fn, fe = arrays[0], arrays[1]
    nodes, w = fn.shape[1], fn.shape[2]
    edges = fe.shape[1]
    halo_rows = arrays[5].shape[2]
    c_edges = arrays[7].shape[1]
    coarse = nodes // 16
    far = pl.BlockSpec(memory_space=pl.ANY)
    near = pl.BlockSpec(memory_space=pltpu.VMEM)
    specs = [near if i == 4 else far for i in range(17)]
    V = pltpu.VMEM
    D = pltpu.SemaphoreType.DMA
    scratch = [
        V((1, edges), jnp.int32),
        V((1, edges), jnp.int32),
        V((1, 4, halo_rows), jnp.int32),
        V((1, nodes), jnp.int32),
        V((1, c_edges), jnp.int32),
        V((1, c_edges), jnp.int32),
        V((2, w), BF),
        V((2, w), BF),
        V((nodes, w), BF),
        V((edges, w), BF),
        V((2, 3 * w, w), BF),
        V((2, w, w), BF),
        V((2, 2 * w, w), BF),
        V((2, w, w), BF),
        V((w, w), BF),
        V((c_edges, w), BF),
        V((nodes, w), BF),
        V((nodes, w), BF),
        V((4, halo_rows, w), BF),
        V((4, halo_rows, w), BF),
        V((edges, w), F32),
        V((edges, 128), jnp.int16),
        V((edges, 128), jnp.int16),
        V((nodes, w), F32),
        V((nodes, w), BF),
        V((2, coarse, w), BF),
        V((2, coarse, w), BF),
        V((NX, NZ, coarse, w), BF),
        V((NX, NZ, coarse, w), BF),
        V((2, c_edges, w), BF),
        V((2, c_edges, w), BF),
        V((coarse, w), BF),
        V((2 * c_edges, 128), jnp.int16),
        V((1, c_edges), jnp.int32),
        V((2 * c_edges, NX * NZ * coarse), BF),
        V((4, coarse, w), BF),
        V((nodes, w), BF),
        D((12,)),
        D((8,)),
        D((2,)),
        D((4,)),
        D((4,)),
        D((2,)),
        D((2,)),
        D((2, 40)),
        D((2, 40)),
        D((2,)),
        D((2,)),
    ]
    return pl.pallas_call(
        kernel,
        out_shape=jax.ShapeDtypeStruct((1, nodes, w), BF),
        in_specs=specs,
        out_specs=far,
        scratch_shapes=scratch,
        compiler_params=pltpu.CompilerParams(
            collective_id=0, has_side_effects=True, vmem_limit_bytes=56 * 1024 * 1024
        ),
        cost_estimate=pl.CostEstimate(
            flops=9_000_000_000, bytes_accessed=12_000_000, transcendentals=2_000_000
        ),
    )(*arrays)


def solution(mesh):
    row = P("dom", "sub")
    wide = P("dom", "sub", None)
    placed = (
        wide, wide, row, row, row, wide, row, wide, row, row,
        P(), P(), P(), P(), P(), P(), P(),
    )
    return jax.shard_map(
        per_device, mesh=mesh, in_specs=placed, out_specs=wide, check_vma=False
    )
```

```python
import functools

import jax
import jax.numpy as jnp
from jax import lax
from jax.experimental import pallas as pl
from jax.experimental.pallas import tpu as pltpu
from jax.sharding import PartitionSpec as P

EPSILON = 1e-05
BF = jnp.bfloat16
F32 = jnp.float32
MESH = pl.DeviceIdType.MESH
ORDER = (0, -1, 1, -2, 2, -3, 3, -4)
NX, NZ = 4, 8
GROUPS = ((0, 1), (1, 5), (5, 8))


def dot(a, b):
    return jnp.dot(a, b, preferred_element_type=F32)


def silu(v):
    half = 0.5 * v
    return half + half * jnp.tanh(half)


def centred(weight):
    wide = weight.astype(F32)
    return (wide - jnp.mean(wide, axis=-1, keepdims=True)).astype(BF)


def scaled(centre, gain):
    variance = jnp.mean(centre * centre, axis=-1, keepdims=True)
    return centre * lax.rsqrt(variance + EPSILON) * gain


def column_of(row):
    n = row.shape[1]
    parts = [
        jnp.transpose(jnp.broadcast_to(row[:, i : i + 128], (128, 128))) for i in range(0, n, 128)
    ]
    return (parts[0] if len(parts) == 1 else jnp.concatenate(parts, axis=0)).astype(jnp.int16)


def ones_where(mask):
    return jnp.where(mask, jnp.ones((), BF), jnp.zeros((), BF))


def pick_matrix(col, lanes, offset=0):
    reps = lanes // 128
    wide = col if reps == 1 else jnp.concatenate([col] * reps, axis=1)
    ids = (lax.broadcasted_iota(jnp.int32, wide.shape, 1) + offset).astype(jnp.int16)
    return ones_where(wide == ids)


def sum_matrix(row, rows):
    shape = (rows, row.shape[1])
    rows_of = lax.broadcasted_iota(jnp.int32, shape, 0).astype(jnp.int16)
    return ones_where(jnp.broadcast_to(row.astype(jnp.int16), shape) == rows_of)


def kernel(
    fn, fe, es_far, et_far, eb, sr_far, cm_far, ce, cs_far, ct_far, ef, e2, eg_far, nf, n2, ng_far, lw,
    out,
    es, et, sr, cm, cs, ct, eg, ng,
    states, lat, wef, we2, wnf, wn2, wlw, cev,
    a_own, b_tgt, pick, halo, pre, src_col, tgt_col, node_pre, refined,
    part, part_in, col0, col1, choice, choice_in, own, csrc, cs_other, wants, sb, outv,
    load_sem, label_sem, out_sem, halo_ss, halo_rs, part_ss, part_rs, ag_ss, ag_rs, set_ss, set_rs,
):
    s = lax.axis_index("sub")
    d = lax.axis_index("dom")
    subs = NX * NZ * 2
    x = s // (2 * NZ)
    z = lax.rem(s // 2, NZ)
    c = lax.rem(s, 2)
    s_up, s_down = lax.rem(s + 1, subs), lax.rem(s + subs - 1, subs)
    d_up, d_down = lax.rem(d + 1, 4), lax.rem(d + 3, 4)

    def place(xx, zz, cc):
        return xx * (2 * NZ) + zz * 2 + cc

    xs = [lax.rem(x + k, NX) for k in range(NX)]
    dev_z = {k: place(x, lax.rem(z + k + NZ, NZ), c) for k in (1, -1, 2, -2)}
    dev_x = [place(xs[k], z, c) for k in range(NX)]
    sibling = place(x, z, 1 - c)

    barrier = pltpu.get_barrier_semaphore()
    for partner in (s_up, s_down, *dev_z.values(), dev_x[1], dev_x[2], dev_x[3]):
        pl.semaphore_signal(barrier, inc=1, device_id={"sub": partner}, device_id_type=MESH)
    for partner in (d_up, d_down):
        pl.semaphore_signal(barrier, inc=1, device_id={"dom": partner}, device_id_type=MESH)

    labels = [
        pltpu.make_async_copy(a, b, label_sem.at[i])
        for i, (a, b) in enumerate(
            [
                (sr_far, sr), (es_far, es), (et_far, et), (cs_far, cs),
                (cm_far, cm), (ct_far, ct), (eg_far, eg), (ng_far, ng),
            ]
        )
    ]
    w = states.shape[1]
    pairs = [
        (fn.at[0], states),
        (ef.at[0, w : 2 * w], wef.at[0, w : 2 * w]),
        (ef.at[0, 2 * w : 3 * w], wef.at[0, 2 * w : 3 * w]),
        (ef.at[0, 0:w], wef.at[0, 0:w]),
        (fe.at[0], lat),
        (nf.at[0], wnf.at[0]),
        (e2, we2),
        (n2, wn2),
        (ce.at[0], cev),
        (ef.at[1], wef.at[1]),
        (nf.at[1], wnf.at[1]),
        (lw, wlw),
    ]
    loads = [pltpu.make_async_copy(a, b, load_sem.at[i]) for i, (a, b) in enumerate(pairs)]
    for copy in labels[:3] + loads[:2] + labels[3:] + loads[2:]:
        copy.start()

    nodes = states.shape[0]
    halo_rows = halo.shape[1]
    coarse = own.shape[0]
    c_edges = cev.shape[0]

    def remote(src, dst, ss, rs, sub=None, dom=None):
        device = {"sub": sub} if dom is None else {"dom": dom}
        return pltpu.make_async_remote_copy(
            src_ref=src, dst_ref=dst, send_sem=ss, recv_sem=rs,
            device_id=device, device_id_type=MESH,
        )

    for copy in labels[:3]:
        copy.wait()
    listed = jnp.concatenate([column_of(sr[0, k : k + 1, :]) for k in range(4)], axis=0)
    wanted = pick_matrix(listed, nodes)
    tgt_col[...] = column_of(et[...])
    src_col[...] = column_of(es[...])
    loads[0].wait()
    loads[1].wait()
    a_own[...] = dot(states[...], wef[0, w : 2 * w]).astype(BF)
    picked = dot(wanted, a_own[...]).astype(BF)
    pick[...] = picked.reshape(4, halo_rows, w)
    for copy in labels[3:]:
        copy.wait()
    pl.semaphore_wait(barrier, 11)
    halo_copies = [
        remote(pick.at[1], halo.at[0], halo_ss.at[0], halo_rs.at[0], sub=s_up),
        remote(pick.at[0], halo.at[1], halo_ss.at[1], halo_rs.at[1], sub=s_down),
        remote(pick.at[3], halo.at[2], halo_ss.at[2], halo_rs.at[2], dom=d_up),
        remote(pick.at[2], halo.at[3], halo_ss.at[3], halo_rs.at[3], dom=d_down),
    ]
    for copy in halo_copies:
        copy.start()
    cs_copy = remote(cs, cs_other, ag_ss.at[0, 21], ag_rs.at[0, 21], sub=sibling)
    cs_copy.start()

    loads[2].wait()
    b_tgt[...] = dot(states[...], wef[0, 2 * w : 3 * w]).astype(BF)
    edges = lat.shape[0]
    loads[3].wait()
    loads[4].wait()
    blocks = edges // nodes

    def first(b, carry):
        here = pl.ds(pl.multiple_of(b * nodes, nodes), nodes)
        pre[here, :] = (
            dot(lat[here, :], wef[0, 0:w])
            + dot(pick_matrix(src_col[here, :], nodes), a_own[...])
            + dot(pick_matrix(tgt_col[here, :], nodes), b_tgt[...])
        )
        return carry

    lax.fori_loop(0, blocks, first, 0, unroll=True)
    loads[5].wait()
    node_pre[...] = dot(states[...], wnf[0, 0:w])
    loads[6].wait()
    we2[0] = centred(we2[0])
    loads[7].wait()
    wn2[0] = centred(wn2[0])

    for copy in halo_copies:
        copy.wait()
    exists = (s > 0, s < subs - 1, d > 0, d < 3)
    for k in range(4):
        halo[k] = jnp.where(exists[k], halo[k].astype(F32), 0.0).astype(BF)
    edge_gain = eg[...].astype(F32)
    node_gain = ng[...].astype(F32)
    used = eb[...]

    def second(b, carry):
        start = pl.multiple_of(b * nodes, nodes)
        here = pl.ds(start, nodes)
        table = halo[...].reshape(4 * halo_rows, w)
        v = pre[here, :] + dot(pick_matrix(src_col[here, :], 4 * halo_rows, nodes), table)
        message = scaled(dot(silu(v).astype(BF), we2[0]), edge_gain[0:1])
        lat[here, :] = (lat[here, :].astype(F32) + message).astype(BF)
        return carry

    lax.fori_loop(0, blocks, second, 0, unroll=True)

    block = lax.broadcasted_iota(jnp.int32, (1, edges), 1) // nodes
    targets = jnp.where(block < used, et[...], -1)
    summed = dot(sum_matrix(targets, nodes), lat[...]).astype(BF)
    v = node_pre[...] + dot(summed, wnf[0, w : 2 * w])
    update = scaled(dot(silu(v).astype(BF), wn2[0]), node_gain[0:1])
    refined[...] = (states[...].astype(F32) + update).astype(BF)
    slots = cm[...] - (s - 1) * coarse
    partial = dot(sum_matrix(slots, 3 * coarse), refined[...])
    part[0] = partial[0:coarse].astype(BF)
    part[1] = partial[2 * coarse : 3 * coarse].astype(BF)
    part_copies = [
        remote(part.at[0], part_in.at[0], part_ss.at[0], part_rs.at[0], sub=s_down),
        remote(part.at[1], part_in.at[1], part_ss.at[1], part_rs.at[1], sub=s_up),
    ]
    for copy in part_copies:
        copy.start()
    csrc[0:c_edges, :] = column_of(cs[...])
    cs_copy.wait()
    csrc[c_edges:, :] = column_of(cs_other[...])
    tgt_pick = ones_where(
        column_of(ct[...])[:, 0:coarse]
        == lax.broadcasted_iota(jnp.int32, (c_edges, coarse), 1).astype(jnp.int16)
    )
    tgt_sum = sum_matrix(ct[...], coarse)
    for i in (8, 9, 10, 11):
        loads[i].wait()
    for copy in part_copies:
        copy.wait()
    own[...] = (
        0.25
        * (
            partial[coarse : 2 * coarse]
            + part_in[0].astype(F32)
            + part_in[1].astype(F32)
        )
    ).astype(BF)

    def gather_parts(g, col):
        ss = lambda i: ag_ss.at[g, i]
        rs = lambda i: ag_rs.at[g, i]

        def send(src, dst, i, target):
            return remote(src, dst, ss(i), rs(i), sub=target)

        def arrived(i, ref):
            remote(ref, ref, ss(i), rs(i), sub=sibling).wait_recv()

        def lines(k, q):
            return col.at[k, GROUPS[q][0] : GROUPS[q][1]]

        def z_send(k, i, step):
            offset = ORDER[i] - step
            to = ORDER.index(offset if offset < 4 else -4)
            return send(col.at[k, i], col.at[k, to], (32 if k else 0) + to, dev_z[step])

        def z_near(k):
            return [z_send(k, 0, step) for step in (2, -2, 1, -1)]

        def z_beyond(k, i):
            if i == 3:
                steps = (1,) if k else (2, 1)
            else:
                steps = (-2, -1) if k else (-1,)
            return [z_send(k, i, step) for step in steps]

        def x_sends(q):
            return [
                send(lines(0, q), lines(3, q), 8 + q, dev_x[1]),
                send(lines(0, q), lines(1, q), 12 + q, dev_x[3]),
            ]

        def x_far():
            return [send(col.at[0, 0], col.at[2, 0], 24, dev_x[2])]

        def choice_send():
            return [send(choice.at[g], choice_in.at[g], 20, sibling)]

        def start(copies):
            for copy in copies:
                copy.start()

        def z_arrived(k, i):
            arrived((32 if k else 0) + i, col.at[k, i])

        def begin():
            start(x_far() + z_near(0) + x_sends(0))

        def forward():
            for i in (3, 4):
                z_arrived(0, i)
                start(z_beyond(0, i))
            for i in (1, 2):
                z_arrived(0, i)
            start(x_sends(1))
            arrived(24, col.at[2, 0])
            start(z_near(2))
            for i in (5, 6, 7):
                z_arrived(0, i)
            start(x_sends(2))
            for i in (3, 4):
                z_arrived(2, i)
                start(z_beyond(2, i))

        def beside():
            for q in range(3):
                arrived(8 + q, lines(3, q))
                arrived(12 + q, lines(1, q))

        def far():
            for i in (1, 2, 5, 6, 7):
                z_arrived(2, i)

        def exchange(theirs):
            choice[g] = theirs
            start(choice_send())

        def exchanged():
            arrived(20, choice_in.at[g])
            return choice_in[g]

        def finish():
            copies = x_far() + choice_send()
            for q in range(3):
                copies += x_sends(q)
            for k in (0, 2):
                copies += z_near(k) + z_beyond(k, 3) + z_beyond(k, 4)
            for copy in copies:
                copy.wait_send()

        return begin, forward, beside, far, exchange, exchanged, finish

    lane = lax.broadcasted_iota(jnp.int32, (1, NZ * coarse), 1)
    turn = lane // coarse
    ahead = jnp.where(lax.rem(turn, 2) == 1, -((turn + 1) // 2), turn // 2)
    span = 2 * coarse
    plane = NZ * coarse
    line_ids = lax.rem(z + ahead + NZ, NZ) * span + c * coarse + lax.rem(lane, coarse)

    finishes = []
    for g, col in enumerate((col0, col1)):
        begin, forward, beside, far, exchange, exchanged, finish = gather_parts(g, col)
        mine = own[...]
        col[0, 0] = mine
        begin()
        picked_own = dot(tgt_pick, mine).astype(BF)
        c_pre = dot(cev[...], wef[1, 0:w]) + dot(picked_own, wef[1, 2 * w : 3 * w])
        n_pre = dot(mine, wnf[1, 0:w])

        forward()
        if g == 0:
            we2[1] = centred(we2[1])
            wn2[1] = centred(wn2[1])
            labels = jnp.concatenate([csrc[...]] * (plane // 128), axis=1)
            for k in range(NX):
                ids = (line_ids + xs[k] * (NZ * span)).astype(jnp.int16)
                wants[:, k * plane : (k + 1) * plane] = ones_where(labels == ids)
        fetched = dot(wants[:, 0:plane], col[0].reshape(plane, w))
        beside()
        far()
        others = col[1:NX].reshape((NX - 1) * plane, w)
        exchange((fetched[c_edges:] + dot(wants[c_edges:, plane:], others)).astype(BF))
        fetched = (fetched[0:c_edges] + dot(wants[0:c_edges, plane:], others)).astype(BF)
        c_pre += dot(fetched, wef[1, w : 2 * w])
        v = c_pre + dot(exchanged(), wef[1, w : 2 * w])
        message = scaled(dot(silu(v).astype(BF), we2[1]), edge_gain[1:2])
        new_edges = (cev[...].astype(F32) + message).astype(BF)
        cev[...] = new_edges
        summed = dot(tgt_sum, new_edges).astype(BF)
        v = n_pre + dot(summed, wnf[1, w : 2 * w])
        update = scaled(dot(silu(v).astype(BF), wn2[1]), node_gain[1:2])
        own[...] = (mine.astype(F32) + update).astype(BF)
        finishes.append(finish)

    sb[1] = own[...]
    sb[3] = jnp.zeros_like(sb[3])
    set_copies = [
        remote(sb.at[1], sb.at[0], set_ss.at[0], set_rs.at[0], sub=s_up),
        remote(sb.at[1], sb.at[2], set_ss.at[1], set_rs.at[1], sub=s_down),
    ]
    for copy in set_copies:
        copy.start()
    chosen = pick_matrix(column_of(slots), 4 * coarse)
    for finish in finishes:
        finish()
    for copy in set_copies:
        copy.wait()
    lifted = dot(sb[...].reshape(4 * coarse, w), wlw[...])
    high = lifted.astype(BF)
    low = (lifted - high.astype(F32)).astype(BF)
    halves = []
    for i in range(2):
        rows = slice(i * (nodes // 2), (i + 1) * (nodes // 2))
        outv[rows, :] = (
            refined[rows, :].astype(F32) + dot(chosen[rows], high) + dot(chosen[rows], low)
        ).astype(BF)
        halves.append(pltpu.make_async_copy(outv.at[rows], out.at[0, rows], out_sem.at[i]))
        halves[i].start()
    for copy in halves:
        copy.wait()


def per_device(*arrays):
    fn, fe = arrays[0], arrays[1]
    nodes, w = fn.shape[1], fn.shape[2]
    edges = fe.shape[1]
    halo_rows = arrays[5].shape[2]
    c_edges = arrays[7].shape[1]
    coarse = nodes // 16
    far = pl.BlockSpec(memory_space=pl.ANY)
    near = pl.BlockSpec(memory_space=pltpu.VMEM)
    specs = [near if i == 4 else far for i in range(17)]
    V = pltpu.VMEM
    D = pltpu.SemaphoreType.DMA
    scratch = [
        V((1, edges), jnp.int32),
        V((1, edges), jnp.int32),
        V((1, 4, halo_rows), jnp.int32),
        V((1, nodes), jnp.int32),
        V((1, c_edges), jnp.int32),
        V((1, c_edges), jnp.int32),
        V((2, w), BF),
        V((2, w), BF),
        V((nodes, w), BF),
        V((edges, w), BF),
        V((2, 3 * w, w), BF),
        V((2, w, w), BF),
        V((2, 2 * w, w), BF),
        V((2, w, w), BF),
        V((w, w), BF),
        V((c_edges, w), BF),
        V((nodes, w), BF),
        V((nodes, w), BF),
        V((4, halo_rows, w), BF),
        V((4, halo_rows, w), BF),
        V((edges, w), F32),
        V((edges, 128), jnp.int16),
        V((edges, 128), jnp.int16),
        V((nodes, w), F32),
        V((nodes, w), BF),
        V((2, coarse, w), BF),
        V((2, coarse, w), BF),
        V((NX, NZ, coarse, w), BF),
        V((NX, NZ, coarse, w), BF),
        V((2, c_edges, w), BF),
        V((2, c_edges, w), BF),
        V((coarse, w), BF),
        V((2 * c_edges, 128), jnp.int16),
        V((1, c_edges), jnp.int32),
        V((2 * c_edges, NX * NZ * coarse), BF),
        V((4, coarse, w), BF),
        V((nodes, w), BF),
        D((12,)),
        D((8,)),
        D((2,)),
        D((4,)),
        D((4,)),
        D((2,)),
        D((2,)),
        D((2, 40)),
        D((2, 40)),
        D((2,)),
        D((2,)),
    ]
    return pl.pallas_call(
        kernel,
        out_shape=jax.ShapeDtypeStruct((1, nodes, w), BF),
        in_specs=specs,
        out_specs=far,
        scratch_shapes=scratch,
        compiler_params=pltpu.CompilerParams(
            collective_id=0, has_side_effects=True, vmem_limit_bytes=56 * 1024 * 1024
        ),
        cost_estimate=pl.CostEstimate(
            flops=9_000_000_000, bytes_accessed=12_000_000, transcendentals=2_000_000
        ),
    )(*arrays)


def solution(mesh):
    row = P("dom", "sub")
    wide = P("dom", "sub", None)
    placed = (
        wide, wide, row, row, row, wide, row, wide, row, row,
        P(), P(), P(), P(), P(), P(), P(),
    )
    return jax.shard_map(
        per_device, mesh=mesh, in_specs=placed, out_specs=wide, check_vma=False
    )
```

```python
import functools

import jax
import jax.numpy as jnp
from jax import lax
from jax.experimental import pallas as pl
from jax.experimental.pallas import tpu as pltpu
from jax.sharding import PartitionSpec as P

EPSILON = 1e-05
BF = jnp.bfloat16
F32 = jnp.float32
MESH = pl.DeviceIdType.MESH
ORDER = (0, -1, 1, -2, 2, -3, 3, -4)
NX, NZ = 4, 8
GROUPS = ((0, 1), (1, 5), (5, 8))


def dot(a, b):
    return jnp.dot(a, b, preferred_element_type=F32)


def silu(v):
    half = 0.5 * v
    return half + half * jnp.tanh(half)


def centred(weight):
    wide = weight.astype(F32)
    return (wide - jnp.mean(wide, axis=-1, keepdims=True)).astype(BF)


def scaled(centre, gain):
    variance = jnp.mean(centre * centre, axis=-1, keepdims=True)
    return centre * lax.rsqrt(variance + EPSILON) * gain


def column_of(row):
    n = row.shape[1]
    parts = [
        jnp.transpose(jnp.broadcast_to(row[:, i : i + 128], (128, 128))) for i in range(0, n, 128)
    ]
    return (parts[0] if len(parts) == 1 else jnp.concatenate(parts, axis=0)).astype(jnp.int16)


def ones_where(mask):
    return jnp.where(mask, jnp.ones((), BF), jnp.zeros((), BF))


def pick_matrix(col, lanes, offset=0):
    reps = lanes // 128
    wide = col if reps == 1 else jnp.concatenate([col] * reps, axis=1)
    ids = (lax.broadcasted_iota(jnp.int32, wide.shape, 1) + offset).astype(jnp.int16)
    return ones_where(wide == ids)


def sum_matrix(row, rows):
    shape = (rows, row.shape[1])
    rows_of = lax.broadcasted_iota(jnp.int32, shape, 0).astype(jnp.int16)
    return ones_where(jnp.broadcast_to(row.astype(jnp.int16), shape) == rows_of)


def kernel(
    fn, fe, es_far, et_far, eb, sr_far, cm_far, ce, cs_far, ct_far, ef, e2, eg_far, nf, n2, ng_far, lw,
    out,
    es, et, sr, cm, cs, ct, eg, ng,
    states, lat, wef, we2, wnf, wn2, wlw, cev,
    pick, halo, pre, src_col, tgt_col, node_pre, refined,
    part, part_in, col0, col1, choice, choice_in, own, csrc, cs_other, sb, outv,
    load_sem, label_sem, out_sem, halo_ss, halo_rs, part_ss, part_rs, ag_ss, ag_rs, set_ss, set_rs,
):
    s = lax.axis_index("sub")
    d = lax.axis_index("dom")
    subs = NX * NZ * 2
    x = s // (2 * NZ)
    z = lax.rem(s // 2, NZ)
    c = lax.rem(s, 2)
    s_up, s_down = lax.rem(s + 1, subs), lax.rem(s + subs - 1, subs)
    d_up, d_down = lax.rem(d + 1, 4), lax.rem(d + 3, 4)

    def place(xx, zz, cc):
        return xx * (2 * NZ) + zz * 2 + cc

    xs = [lax.rem(x + k, NX) for k in range(NX)]
    dev_z = {k: place(x, lax.rem(z + k + NZ, NZ), c) for k in (1, -1, 2, -2)}
    dev_x = [place(xs[k], z, c) for k in range(NX)]
    sibling = place(x, z, 1 - c)

    barrier = pltpu.get_barrier_semaphore()
    for partner in (s_up, s_down, *dev_z.values(), dev_x[1], dev_x[2], dev_x[3]):
        pl.semaphore_signal(barrier, inc=1, device_id={"sub": partner}, device_id_type=MESH)
    for partner in (d_up, d_down):
        pl.semaphore_signal(barrier, inc=1, device_id={"dom": partner}, device_id_type=MESH)

    labels = [
        pltpu.make_async_copy(a, b, label_sem.at[i])
        for i, (a, b) in enumerate(
            [
                (sr_far, sr), (es_far, es), (et_far, et), (cs_far, cs),
                (cm_far, cm), (ct_far, ct), (eg_far, eg), (ng_far, ng),
            ]
        )
    ]
    w = states.shape[1]
    pairs = [
        (fn.at[0], states),
        (ef.at[0, w : 2 * w], wef.at[0, w : 2 * w]),
        (ef.at[0, 2 * w : 3 * w], wef.at[0, 2 * w : 3 * w]),
        (ef.at[0, 0:w], wef.at[0, 0:w]),
        (fe.at[0], lat),
        (nf.at[0], wnf.at[0]),
        (e2, we2),
        (n2, wn2),
        (ce.at[0], cev),
        (ef.at[1], wef.at[1]),
        (nf.at[1], wnf.at[1]),
        (lw, wlw),
    ]
    loads = [pltpu.make_async_copy(a, b, load_sem.at[i]) for i, (a, b) in enumerate(pairs)]
    for copy in labels[:3] + loads[:2] + labels[3:] + loads[2:]:
        copy.start()

    nodes = states.shape[0]
    halo_rows = halo.shape[1]
    coarse = own.shape[0]
    c_edges = cev.shape[0]

    def remote(src, dst, ss, rs, sub=None, dom=None):
        device = {"sub": sub} if dom is None else {"dom": dom}
        return pltpu.make_async_remote_copy(
            src_ref=src, dst_ref=dst, send_sem=ss, recv_sem=rs,
            device_id=device, device_id_type=MESH,
        )

    for copy in labels[:3]:
        copy.wait()
    listed = jnp.concatenate([column_of(sr[0, k : k + 1, :]) for k in range(4)], axis=0)
    wanted = pick_matrix(listed, nodes)
    tgt_col[...] = column_of(et[...])
    src_col[...] = column_of(es[...])
    loads[0].wait()
    loads[1].wait()
    projected = dot(states[...], wef[0, w : 2 * w]).astype(BF)
    picked = dot(wanted, projected).astype(BF)
    wef[0, w : 2 * w] = projected
    pick[...] = picked.reshape(4, halo_rows, w)
    for copy in labels[3:]:
        copy.wait()
    pl.semaphore_wait(barrier, 11)
    halo_copies = [
        remote(pick.at[1], halo.at[0], halo_ss.at[0], halo_rs.at[0], sub=s_up),
        remote(pick.at[0], halo.at[1], halo_ss.at[1], halo_rs.at[1], sub=s_down),
        remote(pick.at[3], halo.at[2], halo_ss.at[2], halo_rs.at[2], dom=d_up),
        remote(pick.at[2], halo.at[3], halo_ss.at[3], halo_rs.at[3], dom=d_down),
    ]
    for copy in halo_copies:
        copy.start()
    cs_copy = remote(cs, cs_other, ag_ss.at[0, 21], ag_rs.at[0, 21], sub=sibling)
    cs_copy.start()

    loads[2].wait()
    wef[0, 2 * w : 3 * w] = dot(states[...], wef[0, 2 * w : 3 * w]).astype(BF)
    edges = lat.shape[0]
    loads[3].wait()
    loads[4].wait()
    blocks = edges // nodes

    def first(b, carry):
        here = pl.ds(pl.multiple_of(b * nodes, nodes), nodes)
        sources = pick_matrix(src_col[here, :], nodes)
        targets = pick_matrix(tgt_col[here, :], nodes)
        pre[here, :] = dot(jnp.concatenate([lat[here, :], sources, targets], axis=1), wef[0])
        return carry

    lax.fori_loop(0, blocks, first, 0, unroll=True)
    loads[5].wait()
    node_pre[...] = dot(states[...], wnf[0, 0:w])
    loads[6].wait()
    we2[0] = centred(we2[0])
    loads[7].wait()
    wn2[0] = centred(wn2[0])

    for copy in halo_copies:
        copy.wait()
    exists = (s > 0, s < subs - 1, d > 0, d < 3)
    for k in range(4):
        halo[k] = jnp.where(exists[k], halo[k].astype(F32), 0.0).astype(BF)
    edge_gain = eg[...].astype(F32)
    node_gain = ng[...].astype(F32)
    used = eb[...]

    def second(b, carry):
        start = pl.multiple_of(b * nodes, nodes)
        here = pl.ds(start, nodes)
        table = halo[...].reshape(4 * halo_rows, w)
        v = pre[here, :] + dot(pick_matrix(src_col[here, :], 4 * halo_rows, nodes), table)
        message = scaled(dot(silu(v).astype(BF), we2[0]), edge_gain[0:1])
        lat[here, :] = (lat[here, :].astype(F32) + message).astype(BF)
        return carry

    lax.fori_loop(0, blocks, second, 0, unroll=True)

    block = lax.broadcasted_iota(jnp.int32, (1, edges), 1) // nodes
    targets = jnp.where(block < used, et[...], -1)
    summed = dot(sum_matrix(targets, nodes), lat[...]).astype(BF)
    v = node_pre[...] + dot(summed, wnf[0, w : 2 * w])
    update = scaled(dot(silu(v).astype(BF), wn2[0]), node_gain[0:1])
    refined[...] = (states[...].astype(F32) + update).astype(BF)
    slots = cm[...] - (s - 1) * coarse
    partial = dot(sum_matrix(slots, 3 * coarse), refined[...])
    part[0] = partial[0:coarse].astype(BF)
    part[1] = partial[2 * coarse : 3 * coarse].astype(BF)
    part_copies = [
        remote(part.at[0], part_in.at[0], part_ss.at[0], part_rs.at[0], sub=s_down),
        remote(part.at[1], part_in.at[1], part_ss.at[1], part_rs.at[1], sub=s_up),
    ]
    for copy in part_copies:
        copy.start()
    csrc[0:c_edges, :] = column_of(cs[...])
    cs_copy.wait()
    csrc[c_edges:, :] = column_of(cs_other[...])
    tgt_pick = ones_where(
        column_of(ct[...])[:, 0:coarse]
        == lax.broadcasted_iota(jnp.int32, (c_edges, coarse), 1).astype(jnp.int16)
    )
    tgt_sum = sum_matrix(ct[...], coarse)
    for i in (8, 9, 10, 11):
        loads[i].wait()
    we2[1] = centred(we2[1])
    wn2[1] = centred(wn2[1])
    for copy in part_copies:
        copy.wait()
    own[...] = (
        0.25
        * (
            partial[coarse : 2 * coarse]
            + part_in[0].astype(F32)
            + part_in[1].astype(F32)
        )
    ).astype(BF)

    def gather_parts(g, col):
        ss = lambda i: ag_ss.at[g, i]
        rs = lambda i: ag_rs.at[g, i]

        def send(src, dst, i, target):
            return remote(src, dst, ss(i), rs(i), sub=target)

        def arrived(i, ref):
            remote(ref, ref, ss(i), rs(i), sub=sibling).wait_recv()

        def lines(k, q):
            return col.at[k, GROUPS[q][0] : GROUPS[q][1]]

        def z_send(k, i, step):
            offset = ORDER[i] - step
            to = ORDER.index(offset if offset < 4 else -4)
            return send(col.at[k, i], col.at[k, to], (32 if k else 0) + to, dev_z[step])

        def z_near(k):
            return [z_send(k, 0, step) for step in (2, -2, 1, -1)]

        def z_beyond(k, i):
            if i == 3:
                steps = (1,) if k else (2, 1)
            else:
                steps = (-2, -1) if k else (-1,)
            return [z_send(k, i, step) for step in steps]

        def x_sends(q):
            return [
                send(lines(0, q), lines(3, q), 8 + q, dev_x[1]),
                send(lines(0, q), lines(1, q), 12 + q, dev_x[3]),
            ]

        def x_far():
            return [send(col.at[0, 0], col.at[2, 0], 24, dev_x[2])]

        def choice_send():
            return [send(choice.at[g], choice_in.at[g], 20, sibling)]

        def start(copies):
            for copy in copies:
                copy.start()

        def z_arrived(k, i):
            arrived((32 if k else 0) + i, col.at[k, i])

        def begin():
            start(x_far() + z_near(0) + x_sends(0))

        def forward():
            for i in (3, 4):
                z_arrived(0, i)
                start(z_beyond(0, i))
            arrived(24, col.at[2, 0])
            start(z_near(2))
            for i in (1, 2):
                z_arrived(0, i)
            start(x_sends(1))
            for i in (5, 6, 7):
                z_arrived(0, i)
            start(x_sends(2))
            for i in (3, 4):
                z_arrived(2, i)
                start(z_beyond(2, i))

        def beside():
            for q in range(3):
                arrived(8 + q, lines(3, q))
                arrived(12 + q, lines(1, q))

        def far():
            for i in (1, 2, 5, 6, 7):
                z_arrived(2, i)

        def exchange(theirs):
            choice[g] = theirs
            start(choice_send())

        def exchanged():
            arrived(20, choice_in.at[g])
            return choice_in[g]

        def finish():
            copies = x_far() + choice_send()
            for q in range(3):
                copies += x_sends(q)
            for k in (0, 2):
                copies += z_near(k) + z_beyond(k, 3) + z_beyond(k, 4)
            for copy in copies:
                copy.wait_send()

        return begin, forward, beside, far, exchange, exchanged, finish

    lane = lax.broadcasted_iota(jnp.int32, (1, NZ * coarse), 1)
    turn = lane // coarse
    ahead = jnp.where(lax.rem(turn, 2) == 1, -((turn + 1) // 2), turn // 2)
    span = 2 * coarse
    line_ids = lax.rem(z + ahead + NZ, NZ) * span + c * coarse + lax.rem(lane, coarse)

    finishes = []
    for g, col in enumerate((col0, col1)):
        begin, forward, beside, far, exchange, exchanged, finish = gather_parts(g, col)
        mine = own[...]
        col[0, 0] = mine
        begin()
        picked_own = dot(tgt_pick, mine).astype(BF)
        c_pre = dot(cev[...], wef[1, 0:w]) + dot(picked_own, wef[1, 2 * w : 3 * w])
        n_pre = dot(mine, wnf[1, 0:w])

        def chosen_rows(k, rows):
            labels = jnp.concatenate([csrc[rows, :]] * (NZ * coarse // 128), axis=1)
            return dot(
                ones_where(labels == (line_ids + xs[k] * (NZ * span)).astype(jnp.int16)),
                col[k].reshape(NZ * coarse, w),
            )

        everyone = slice(0, 2 * c_edges)
        forward()
        fetched = chosen_rows(0, everyone)
        beside()
        fetched += chosen_rows(3, everyone) + chosen_rows(1, everyone)
        far()
        exchange((fetched[c_edges:] + chosen_rows(2, slice(c_edges, 2 * c_edges))).astype(BF))
        fetched = fetched[0:c_edges] + chosen_rows(2, slice(0, c_edges))
        fetched += exchanged().astype(F32)
        v = c_pre + dot(fetched.astype(BF), wef[1, w : 2 * w])
        message = scaled(dot(silu(v).astype(BF), we2[1]), edge_gain[1:2])
        new_edges = (cev[...].astype(F32) + message).astype(BF)
        cev[...] = new_edges
        summed = dot(tgt_sum, new_edges).astype(BF)
        v = n_pre + dot(summed, wnf[1, w : 2 * w])
        update = scaled(dot(silu(v).astype(BF), wn2[1]), node_gain[1:2])
        own[...] = (mine.astype(F32) + update).astype(BF)
        finishes.append(finish)

    sb[1] = own[...]
    sb[3] = jnp.zeros_like(sb[3])
    set_copies = [
        remote(sb.at[1], sb.at[0], set_ss.at[0], set_rs.at[0], sub=s_up),
        remote(sb.at[1], sb.at[2], set_ss.at[1], set_rs.at[1], sub=s_down),
    ]
    for copy in set_copies:
        copy.start()
    chosen = pick_matrix(column_of(slots), 4 * coarse)
    for finish in finishes:
        finish()
    for copy in set_copies:
        copy.wait()
    lifted = dot(sb[...].reshape(4 * coarse, w), wlw[...])
    high = lifted.astype(BF)
    low = (lifted - high.astype(F32)).astype(BF)
    halves = []
    for i in range(2):
        rows = slice(i * (nodes // 2), (i + 1) * (nodes // 2))
        outv[rows, :] = (
            refined[rows, :].astype(F32) + dot(chosen[rows], high) + dot(chosen[rows], low)
        ).astype(BF)
        halves.append(pltpu.make_async_copy(outv.at[rows], out.at[0, rows], out_sem.at[i]))
        halves[i].start()
    for copy in halves:
        copy.wait()


def per_device(*arrays):
    fn, fe = arrays[0], arrays[1]
    nodes, w = fn.shape[1], fn.shape[2]
    edges = fe.shape[1]
    halo_rows = arrays[5].shape[2]
    c_edges = arrays[7].shape[1]
    coarse = nodes // 16
    far = pl.BlockSpec(memory_space=pl.ANY)
    near = pl.BlockSpec(memory_space=pltpu.VMEM)
    specs = [near if i == 4 else far for i in range(17)]
    V = pltpu.VMEM
    D = pltpu.SemaphoreType.DMA
    scratch = [
        V((1, edges), jnp.int32),
        V((1, edges), jnp.int32),
        V((1, 4, halo_rows), jnp.int32),
        V((1, nodes), jnp.int32),
        V((1, c_edges), jnp.int32),
        V((1, c_edges), jnp.int32),
        V((2, w), BF),
        V((2, w), BF),
        V((nodes, w), BF),
        V((edges, w), BF),
        V((2, 3 * w, w), BF),
        V((2, w, w), BF),
        V((2, 2 * w, w), BF),
        V((2, w, w), BF),
        V((w, w), BF),
        V((c_edges, w), BF),
        V((4, halo_rows, w), BF),
        V((4, halo_rows, w), BF),
        V((edges, w), F32),
        V((edges, 128), jnp.int16),
        V((edges, 128), jnp.int16),
        V((nodes, w), F32),
        V((nodes, w), BF),
        V((2, coarse, w), BF),
        V((2, coarse, w), BF),
        V((NX, NZ, coarse, w), BF),
        V((NX, NZ, coarse, w), BF),
        V((2, c_edges, w), BF),
        V((2, c_edges, w), BF),
        V((coarse, w), BF),
        V((2 * c_edges, 128), jnp.int16),
        V((1, c_edges), jnp.int32),
        V((4, coarse, w), BF),
        V((nodes, w), BF),
        D((12,)),
        D((8,)),
        D((2,)),
        D((4,)),
        D((4,)),
        D((2,)),
        D((2,)),
        D((2, 40)),
        D((2, 40)),
        D((2,)),
        D((2,)),
    ]
    return pl.pallas_call(
        kernel,
        out_shape=jax.ShapeDtypeStruct((1, nodes, w), BF),
        in_specs=specs,
        out_specs=far,
        scratch_shapes=scratch,
        compiler_params=pltpu.CompilerParams(
            collective_id=0, has_side_effects=True, vmem_limit_bytes=56 * 1024 * 1024
        ),
        cost_estimate=pl.CostEstimate(
            flops=9_000_000_000, bytes_accessed=12_000_000, transcendentals=2_000_000
        ),
    )(*arrays)


def solution(mesh):
    row = P("dom", "sub")
    wide = P("dom", "sub", None)
    placed = (
        wide, wide, row, row, row, wide, row, wide, row, row,
        P(), P(), P(), P(), P(), P(), P(),
    )
    return jax.shard_map(
        per_device, mesh=mesh, in_specs=placed, out_specs=wide, check_vma=False
    )
```
